32 devices in a mesh: gx: 4 (over y, x), gy: 8 (over z, core).
Axes of the slice: x: 2, y: 2, z: 4, core: 2. Of those that a mesh axis runs over, the one named last changes fastest.
Arguments:
- e_field: float32 [3, 32, 256, 512], P(None, 'gx', 'gy'), may hold values from -6 to 6
- h_field: float32 [3, 32, 256, 512], P(None, 'gx', 'gy'), may hold values from -6 to 6
- polar: float32 [3, 32, 256, 512], P(None, 'gx', 'gy'), may hold values from -6 to 6
- polar_prev: float32 [3, 32, 256, 512], P(None, 'gx', 'gy'), may hold values from -6 to 6
- material: int32 [32, 256, 512], P('gx', 'gy'), may hold values from 0 to 3
- eps_table: float32 [4], replicated, may hold values from 1 to 6
- delta_table: float32 [4], replicated, may hold values from 0.5 to 4
- omega_table: float32 [4], replicated, may hold values from 0.2 to 1.2
- damping_table: float32 [4], replicated, may hold values from 0.02 to 0.6
- surface_flags: int32 [4, 8], P('gx', 'gy'), may hold values 0 or 1
Outputs:
- e_out: float32 [3, 32, 256, 512], P(None, 'gx', 'gy')
- h_out: float32 [3, 32, 256, 512], P(None, 'gx', 'gy')
- polar_out: float32 [3, 32, 256, 512], P(None, 'gx', 'gy')
- far_field: float32 [2, 2, 4, 16384], replicated
The draws below stay inside these ranges and needn't reach their ends.
All inputs are finite; a program needn't handle non-finite values. No bound on the sum of `surface_flags` on one device may be relied on, other than what follows from the above.
Results may differ from the reference program's by a relative error of at most 0.0003.
Values sent between devices are 32-bit elements; how exact they have to be, the bound alone decides.
A program may use at most 256 MiB of HBM per device.

```python
import math
import jax
import jax.numpy as jnp
from jax import lax

CX = 8
CY = 32
NZ = 512
NMAT = 4
NTH = 64
NPH = 256
NDIR = 16384
ZS = 384
NX = 32
NY = 256
STRETCHES_X = 4
STRETCHES_Y = 8


def place_ends(drawn, stream_key, low, largest):
    index_at = [jax.random.randint(jax.random.fold_in(stream_key, axis), (), 0, length) for axis, length in enumerate(drawn.shape)]
    main_axis = drawn.shape.index(max(drawn.shape))
    beside = index_at[:main_axis] + [(index_at[main_axis] + 1) % drawn.shape[main_axis]] + index_at[main_axis + 1:]
    return drawn.at[tuple(index_at)].set(low).at[tuple(beside)].set(largest)


def level_of(own_key, shape, shards, low, largest):
    loudness, own = 1.0, jax.random.fold_in(own_key, 6)
    for dim, blocks in shards:
        draws = jnp.exp(jax.random.uniform(jax.random.fold_in(own, dim), (blocks,), jnp.float32, low / len(shards), largest / len(shards)))
        loudness = loudness * jnp.repeat(draws, shape[dim] // blocks).reshape([-1 if axis == dim else 1 for axis in range(len(shape))])
    return loudness


def centred(rng, shape, width, bound, pieces=(), kind=jnp.bfloat16):
    gain = level_of(rng, shape, pieces, -0.22, 0.18) if pieces else 1.0
    drawn = jax.random.normal(rng, shape, jnp.float32) * width * gain
    return jnp.minimum(jnp.maximum(drawn, -bound), bound).astype(kind)


def setup_inputs(seed: int = 0) -> dict:
    splits = jax.random.split(jax.random.key(seed), 11)
    e_field = centred(splits[0], (3, NX, NY, NZ), 1.0, 6.0, ((1, 4), (2, 8)), jnp.float32)
    h_field = centred(splits[1], (3, NX, NY, NZ), 1.0, 6.0, ((1, 4), (2, 8)), jnp.float32)
    polar = centred(splits[2], (3, NX, NY, NZ), 1.0, 6.0, ((1, 4), (2, 8)), jnp.float32)
    polar_prev = centred(splits[3], (3, NX, NY, NZ), 1.0, 6.0, ((1, 4), (2, 8)), jnp.float32)
    material = place_ends(jax.random.randint(splits[4], (NX, NY, NZ), 0, NMAT), jax.random.fold_in(splits[4], 1), 0, NMAT - 1).astype(jnp.int32)
    eps_table = jnp.clip(jnp.exp(jax.random.uniform(splits[5], (NMAT,), jnp.float32, math.log(1.0), math.log(6.0))), 1.0, 6.0)
    delta_table = jnp.clip(jnp.exp(jax.random.uniform(splits[6], (NMAT,), jnp.float32, math.log(0.5), math.log(4.0))), 0.5, 4.0)
    omega_table = jnp.clip(jnp.exp(jax.random.uniform(splits[7], (NMAT,), jnp.float32, math.log(0.2), math.log(1.2))), 0.2, 1.2)
    damping_table = jnp.clip(jnp.exp(jax.random.uniform(splits[8], (NMAT,), jnp.float32, math.log(0.02), math.log(0.6))), 0.02, 0.6)
    surface_flags = place_ends((jax.random.randint(splits[9], (STRETCHES_X, STRETCHES_Y), 0, 4) < 3).astype(jnp.int32), jax.random.fold_in(splits[9], 1), 0, 1)
    return {"e_field": e_field, "h_field": h_field, "polar": polar, "polar_prev": polar_prev, "material": material, "eps_table": eps_table, "delta_table": delta_table, "omega_table": omega_table, "damping_table": damping_table, "surface_flags": surface_flags}


DT = 0.55
WAVELENGTHS = (5.0, 4.0)

def ahead(field, plane, axis):
    rest = lax.slice_in_dim(field, 1, field.shape[axis], axis=axis)
    return jnp.concatenate([rest, plane], axis=axis) - field

def behind(field, plane, axis):
    rest = lax.slice_in_dim(field, 0, field.shape[axis] - 1, axis=axis)
    return field - jnp.concatenate([plane, rest], axis=axis)

def zero_plane(field, axis):
    shape = list(field.shape)
    shape[axis] = 1
    return jnp.zeros(shape, jnp.float32)

def coefficients(eps_table, delta_table, omega_table, damping_table):
    half = damping_table * (DT / 2.0)
    denom = 1.0 + half
    square = omega_table * omega_table * (DT * DT)
    return ((2.0 - square) / denom, (half - 1.0) / denom, delta_table * square / denom, 1.0 / eps_table)

def curl_e(ex, ey, ez, xnext, ynext):
    zplane = zero_plane(ex, 2)
    curl_x = ahead(ez, ynext[1], 1) - ahead(ey, zplane, 2)
    curl_y = ahead(ex, zplane, 2) - ahead(ez, xnext[1], 0)
    curl_z = ahead(ey, xnext[0], 0) - ahead(ex, ynext[0], 1)
    return (curl_x, curl_y, curl_z)

def curl_h(hx, hy, hz, xprev, yprev):
    zplane = zero_plane(hx, 2)
    curl_x = behind(hz, yprev[1], 1) - behind(hy, zplane, 2)
    curl_y = behind(hx, zplane, 2) - behind(hz, xprev[1], 0)
    curl_z = behind(hy, xprev[0], 0) - behind(hx, yprev[0], 1)
    return (curl_x, curl_y, curl_z)

def directions(start, count):
    index = start + jnp.arange(count, dtype=jnp.int32)
    theta = ((index // NPH).astype(jnp.float32) + 0.5) * (math.pi / 2.0 / NTH)
    phi = ((index % NPH).astype(jnp.float32) + 0.5) * (2.0 * math.pi / NPH)
    return (jnp.sin(theta) * jnp.cos(phi), jnp.sin(theta) * jnp.sin(phi))

def reference(e_field, h_field, polar, polar_prev, material, eps_table, delta_table, omega_table, damping_table, surface_flags):
    coef_a, coef_b, coef_c, coef_inv = coefficients(eps_table, delta_table, omega_table, damping_table)
    vox_a = jnp.take(coef_a, material)
    vox_b = jnp.take(coef_b, material)
    vox_c = jnp.take(coef_c, material)
    vox_inv = jnp.take(coef_inv, material)
    flags = jnp.repeat(jnp.repeat(surface_flags, CX, 0), CY, 1).astype(jnp.float32)
    ex, ey, ez = (e_field[0], e_field[1], e_field[2])
    hx, hy, hz = (h_field[0], h_field[1], h_field[2])
    pols = [polar[0], polar[1], polar[2]]
    prevs = [polar_prev[0], polar_prev[1], polar_prev[2]]
    xz = zero_plane(ex, 0)
    yz = zero_plane(ex, 1)
    real_acc = jnp.zeros((2, 4, NX, NY), jnp.float32)
    imag_acc = jnp.zeros((2, 4, NX, NY), jnp.float32)
    for step in range(2):
        curl_x, curl_y, curl_z = curl_e(ex, ey, ez, (xz, xz), (yz, yz))
        hx = hx - DT * curl_x
        hy = hy - DT * curl_y
        hz = hz - DT * curl_z
        fields = [ex, ey, ez]
        newpol = [vox_a * pols[i] + vox_b * prevs[i] + vox_c * fields[i] for i in range(3)]
        curls = curl_h(hx, hy, hz, (xz, xz), (yz, yz))
        fields = [fields[i] + (DT * curls[i] - (newpol[i] - pols[i])) * vox_inv for i in range(3)]
        ex, ey, ez = fields
        prevs = pols
        pols = newpol
        surface = jnp.stack([-hy[:, :, ZS], hx[:, :, ZS], ey[:, :, ZS], -ex[:, :, ZS]]) * flags[None]
        moment = (step + 1) * DT
        real_acc = real_acc + jnp.stack([surface * math.cos(2.0 * math.pi / WAVELENGTHS[f] * moment) for f in range(2)])
        imag_acc = imag_acc - jnp.stack([surface * math.sin(2.0 * math.pi / WAVELENGTHS[f] * moment) for f in range(2)])
    dir_x, dir_y = directions(0, NDIR)
    ypos = jnp.arange(NY).astype(jnp.float32)

    def row(total, item):
        xpos, real_row, imag_row = item
        parts = []
        for f in range(2):
            wave = 2.0 * math.pi / WAVELENGTHS[f]
            phase = wave * (xpos * dir_x[None, :] + ypos[:, None] * dir_y[None, :])
            cosine = jnp.cos(phase)
            sine = jnp.sin(phase)
            hi = lax.Precision.HIGHEST
            real_part = jnp.dot(real_row[f], cosine, precision=hi) - jnp.dot(imag_row[f], sine, precision=hi)
            imag_part = jnp.dot(real_row[f], sine, precision=hi) + jnp.dot(imag_row[f], cosine, precision=hi)
            parts.append(jnp.stack([real_part, imag_part]))
        return (total + jnp.stack(parts), None)
    rows_x = jnp.arange(NX).astype(jnp.float32)
    total, unused = lax.scan(row, jnp.zeros((2, 2, 4, NDIR), jnp.float32), (rows_x, jnp.moveaxis(real_acc, 2, 0), jnp.moveaxis(imag_acc, 2, 0)))
    far_field = total * (1.0 / math.sqrt(NX * NY))
    return (jnp.stack([ex, ey, ez]), jnp.stack([hx, hy, hz]), jnp.stack(pols), far_field)
```

```python
import functools
import math

import jax
import jax.numpy as jnp
import numpy as np
from jax import lax
from jax.experimental import pallas as pl
from jax.experimental.pallas import tpu as pltpu
from jax.sharding import PartitionSpec as P

NTH = 64
NPH = 256
NDIR = 16384
ZS = 384
DT = 0.55
WAVELENGTHS = (5.0, 4.0)
MESH = pl.DeviceIdType.MESH
F32 = jnp.float32
BF16 = jnp.bfloat16
BY = 8


def coefficients(nmat, nz, eps, delta, omega, damping):
    coef = []
    for m in range(nmat):
        half = jnp.full((1, nz), damping[m], F32) * (DT / 2.0)
        denom = 1.0 + half
        om = jnp.full((1, nz), omega[m], F32)
        square = om * om * (DT * DT)
        coef.append((
            (2.0 - square) / denom,
            (half - 1.0) / denom,
            jnp.full((1, nz), delta[m], F32) * square / denom,
            1.0 / jnp.full((1, nz), eps[m], F32),
        ))
    return coef


def step_kernel(
    ngx, ngy, nmat,
    e_in, h_in, p_in, q_in, m_in, eps_in, delta_in, omega_in, damping_in, flags_in,
    e_out, h_out, p_out, g_out,
    E, H, PA, PB, MAT, ystage, ye, yh, G, eps, delta, omega, damping, flags,
    in_sem, out_sem, xs_sem, xr_sem, ys_sem, yr_sem, g1s, g1r, all_in,
):
    cx, cy, nz = MAT.shape
    gx = lax.axis_index("gx")
    gy = lax.axis_index("gy")

    loads = [
        pltpu.make_async_copy(e_in, E.at[:, pl.ds(0, cx)], in_sem.at[0]),
        pltpu.make_async_copy(h_in, H.at[:, pl.ds(1, cx)], in_sem.at[1]),
        pltpu.make_async_copy(p_in, PA, in_sem.at[2]),
        pltpu.make_async_copy(q_in, PB, in_sem.at[3]),
        pltpu.make_async_copy(m_in, MAT, in_sem.at[4]),
        pltpu.make_async_copy(eps_in, eps, in_sem.at[5]),
        pltpu.make_async_copy(delta_in, delta, in_sem.at[6]),
        pltpu.make_async_copy(omega_in, omega, in_sem.at[7]),
        pltpu.make_async_copy(damping_in, damping, in_sem.at[8]),
        pltpu.make_async_copy(flags_in, flags, in_sem.at[9]),
    ]
    for load in loads:
        load.start()

    barrier = pltpu.get_barrier_semaphore()
    for k in range(1, ngx):
        pl.semaphore_signal(barrier, inc=1, device_id=(lax.rem(gx + k, ngx), gy), device_id_type=MESH)
    for k in range(1, ngy):
        pl.semaphore_signal(barrier, inc=1, device_id=(gx, lax.rem(gy + k, ngy)), device_id_type=MESH)

    @pl.when(gx == ngx - 1)
    def _():
        for c in (1, 2):
            E[c, cx] = jnp.zeros((cy, nz), F32)

    @pl.when(gx == 0)
    def _():
        for c in (1, 2):
            H[c, 0] = jnp.zeros((cy, nz), F32)

    @pl.when(gy == ngy - 1)
    def _():
        ye[...] = jnp.zeros(ye.shape, F32)

    @pl.when(gy == 0)
    def _():
        yh[...] = jnp.zeros(yh.shape, F32)

    def copies(rnd, step):
        if rnd % 2 == 0:
            field, at_src, at_dst, ydst = E, 0, cx, ye.at[step]
            tx, ty = gx - 1, gy - 1
            sends_x, sends_y = gx > 0, gy > 0
            takes_x, takes_y = gx < ngx - 1, gy < ngy - 1
        else:
            field, at_src, at_dst, ydst = H, cx, 0, yh.at[step]
            tx, ty = gx + 1, gy + 1
            sends_x, sends_y = gx < ngx - 1, gy < ngy - 1
            takes_x, takes_y = gx > 0, gy > 0
        xcopies = []
        for i in range(2 * (cy // BY)):
            c, y = 1 + i % 2, (i // 2) * BY
            xcopies.append(pltpu.make_async_remote_copy(
                src_ref=field.at[c, at_src, pl.ds(y, BY)], dst_ref=field.at[c, at_dst, pl.ds(y, BY)],
                send_sem=xs_sem.at[rnd, i], recv_sem=xr_sem.at[rnd, i],
                device_id=(lax.rem(tx + ngx, ngx), gy), device_id_type=MESH))
        ycopy = pltpu.make_async_remote_copy(
            src_ref=ystage.at[rnd], dst_ref=ydst, send_sem=ys_sem.at[rnd], recv_sem=yr_sem.at[rnd],
            device_id=(gx, lax.rem(ty + ngy, ngy)), device_id_type=MESH)
        return xcopies, ycopy, sends_x, sends_y, takes_x, takes_y

    def send_x(rnd, step, block):
        xcopies, _, sends_x, _, _, _ = copies(rnd, step)

        @pl.when(sends_x)
        def _():
            for xcopy in xcopies[2 * block : 2 * block + 2]:
                xcopy.start()

    def send_y(rnd, step):
        _, ycopy, _, sends_y, _, _ = copies(rnd, step)
        for i, c in enumerate((0, 2)):
            for x in range(cx):
                if rnd % 2 == 0:
                    ystage[rnd, i, x : x + 1, :] = E[c, x, 0:1, :]
                else:
                    ystage[rnd, i, x : x + 1, :] = H[c, x + 1, cy - 1 : cy, :]
        pl.when(sends_y)(ycopy.start)

    def take_x(rnd, step, block):
        xcopies, _, _, _, takes_x, _ = copies(rnd, step)

        @pl.when(takes_x)
        def _():
            for xcopy in xcopies[2 * block : 2 * block + 2]:
                xcopy.wait_recv()

    def take_y(rnd, step):
        _, ycopy, _, _, _, takes_y = copies(rnd, step)
        pl.when(takes_y)(ycopy.wait_recv)

    def sent_x(rnd, step):
        xcopies, _, sends_x, _, _, _ = copies(rnd, step)

        @pl.when(sends_x)
        def _():
            for xcopy in xcopies:
                xcopy.wait_send()

    def sent_y(rnd, step):
        _, ycopy, _, sends_y, _, _ = copies(rnd, step)
        pl.when(sends_y)(ycopy.wait_send)

    row_id = lax.broadcasted_iota(jnp.int32, (BY, nz), 0)
    lane_id = lax.broadcasted_iota(jnp.int32, (BY, nz), 1)

    def up_y(v, row):
        return jnp.where(row_id == BY - 1, row, pltpu.roll(v, BY - 1, 0))

    def up_z(v):
        return jnp.where(lane_id == nz - 1, 0.0, pltpu.roll(v, nz - 1, 1))

    def down_y(v, row):
        return jnp.where(row_id == 0, row, pltpu.roll(v, 1, 0))

    def down_z(v):
        return jnp.where(lane_id == 0, 0.0, pltpu.roll(v, 1, 1))

    def h_plane(step, x, blocks):
        for y in [BY * block for block in blocks]:
            here = pl.ds(y, BY)
            ex, ey, ez = E[0, x, here, :], E[1, x, here, :], E[2, x, here, :]
            if y + BY < cy:
                rx, rz = E[0, x, y + BY : y + BY + 1, :], E[2, x, y + BY : y + BY + 1, :]
            else:
                rx, rz = ye[step, 0, pl.ds(x, 1), :], ye[step, 1, pl.ds(x, 1), :]
            eyx, ezx = E[1, x + 1, here, :], E[2, x + 1, here, :]
            curl_x = (up_y(ez, rz) - ez) - (up_z(ey) - ey)
            curl_y = (up_z(ex) - ex) - (ezx - ez)
            curl_z = (eyx - ey) - (up_y(ex, rx) - ex)
            H[0, x + 1, here, :] = H[0, x + 1, here, :] - DT * curl_x
            H[1, x + 1, here, :] = H[1, x + 1, here, :] - DT * curl_y
            H[2, x + 1, here, :] = H[2, x + 1, here, :] - DT * curl_z

    def e_plane(step, x, coef, blocks):
        now, old = (PA, PB) if step == 0 else (PB, PA)
        for y in [BY * block for block in blocks]:
            here = pl.ds(y, BY)
            mat = MAT[x, here, :]
            vox = [jnp.broadcast_to(coef[nmat - 1][i], (BY, nz)) for i in range(4)]
            for m in range(nmat - 1):
                hit = mat == m
                vox = [jnp.where(hit, coef[m][i], vox[i]) for i in range(4)]
            a, b, c, inv = vox
            hx, hy, hz = H[0, x + 1, here, :], H[1, x + 1, here, :], H[2, x + 1, here, :]
            if y > 0:
                rx, rz = H[0, x + 1, y - 1 : y, :], H[2, x + 1, y - 1 : y, :]
            else:
                rx, rz = yh[step, 0, pl.ds(x, 1), :], yh[step, 1, pl.ds(x, 1), :]
            hyx, hzx = H[1, x, here, :], H[2, x, here, :]
            curls = (
                (hz - down_y(hz, rz)) - (hy - down_z(hy)),
                (hx - down_z(hx)) - (hz - hzx),
                (hy - hyx) - (hx - down_y(hx, rx)),
            )
            for i in range(3):
                e, p = E[i, x, here, :], now[i, x, here, :]
                new = a * p + b * old[i, x, here, :] + c * e
                E[i, x, here, :] = e + (DT * curls[i] - (new - p)) * inv
                old[i, x, here, :] = new

    me = gx * ngy + gy
    count = ngx * ngy
    turn_x, turn_y = 2 * gx >= ngx, 2 * gy >= ngy
    tile_lane = lax.broadcasted_iota(jnp.int32, (8, 128), 1)
    tile_row = lax.broadcasted_iota(jnp.int32, (8, 128), 0)

    def surface(step, flag):
        def body(x, acc):
            at = jnp.where(turn_x, cx - 1 - x, x) * 4
            for yb in range(cy // 8):
                base = jnp.where(turn_y, cy // 8 - 1 - yb, yb) * (4 * cx) + at
                rows = slice(8 * yb, 8 * yb + 8)
                cols = (
                    -H[1, x + 1, rows, ZS : ZS + 1], H[0, x + 1, rows, ZS : ZS + 1],
                    E[1, x, rows, ZS : ZS + 1], -E[0, x, rows, ZS : ZS + 1],
                )
                for j in range(4):
                    acc = jnp.where(tile_lane == base + j, cols[j], acc)
            return acc

        tile = lax.fori_loop(0, cx, body, jnp.zeros((8, 128), F32)) * flag
        back = tile
        for bit in (1, 2, 4):
            back = jnp.where((tile_row & bit) != 0, pltpu.roll(back, bit, 0), pltpu.roll(back, 8 - bit, 0))
        G[step] = jnp.where(turn_y, back, tile)

    def peer(step, k):
        to = lax.rem(me + k, count)
        return pltpu.make_async_remote_copy(
            src_ref=G.at[step], dst_ref=g_out.at[step, me], send_sem=g1s.at[step, k], recv_sem=g1r.at[step, k],
            device_id=(to // ngy, lax.rem(to, ngy)), device_id_type=MESH)

    def own(step):
        return pltpu.make_async_copy(G.at[step], g_out.at[step, me], out_sem.at[3 + step])

    def gather_start(step):
        own(step).start()

        @pl.loop(1, count)
        def _(k):
            peer(step, k).start()

    def gather_end(step):
        own(step).wait()

        @pl.loop(1, count)
        def _(k):
            peer(step, k).wait()

    loads[0].wait()
    pl.semaphore_wait(barrier, ngx + ngy - 2)
    for k in range(1, ngy):
        pl.semaphore_signal(all_in, inc=1, device_id=(gx, lax.rem(gy + k, ngy)), device_id_type=MESH)
    blocks = range(cy // BY)
    send_y(0, 0)
    for block in blocks:
        send_x(0, 0, block)
    for load in loads[1:2] + loads[5:]:
        load.wait()

    coef = coefficients(nmat, nz, eps, delta, omega, damping)
    flag = flags[0, 0].astype(F32)

    for step in range(2):
        down, up = 2 * step, 2 * step + 1
        take_y(down, step)

        @pl.loop(0, cx - 1)
        def _(x):
            h_plane(step, x, blocks)

        for block in blocks:
            take_x(down, step, block)
            h_plane(step, cx - 1, [block])
            send_x(up, step, block)
        send_y(up, step)
        if step == 0:
            for load in loads[2:5]:
                load.wait()
        else:
            pltpu.make_async_copy(H.at[:, pl.ds(1, cx)], h_out, out_sem.at[0]).start()
            gather_start(0)
        sent_x(down, step)
        take_y(up, step)

        @pl.loop(1, cx)
        def _(x):
            e_plane(step, x, coef, blocks)

        for block in blocks:
            take_x(up, step, block)
            e_plane(step, 0, coef, [block])
            if step == 0:
                send_x(2, 1, block)
        if step == 0:
            send_y(2, 1)
            sent_x(up, step)
        surface(step, flag)
        if step == 0:
            pl.semaphore_wait(all_in, ngy - 1)
        else:
            gather_start(1)

    saves = [
        pltpu.make_async_copy(H.at[:, pl.ds(1, cx)], h_out, out_sem.at[0]),
        pltpu.make_async_copy(E.at[:, pl.ds(0, cx)], e_out, out_sem.at[1]),
        pltpu.make_async_copy(PA, p_out, out_sem.at[2]),
    ]
    saves[1].start()
    saves[2].start()
    sent_x(3, 1)
    for rnd in range(4):
        sent_y(rnd, rnd // 2)
    gather_end(0)
    gather_end(1)
    for save in saves:
        save.wait()


TILE = 1024
PART = 256
TABLES = 2 * 2 * 2


def angles():
    theta = (np.arange(NTH, dtype=np.float64)[:, None] + 0.5) * (math.pi / 2.0 / NTH)
    phi = (np.arange(NPH // 4, dtype=np.float64)[None, :] + 0.5) * (2.0 * math.pi / NPH)
    ux = (np.sin(theta) * np.cos(phi)).reshape(-1)
    uy = (np.sin(theta) * np.sin(phi)).reshape(-1)
    return ux, uy


def tiled(rows):
    return np.ascontiguousarray(rows.reshape(rows.shape[0], -1, TILE).swapaxes(0, 1))


def make_seeds(nx, ny):
    ux, uy = angles()
    x0, y0 = (nx - 1) / 2.0, (ny - 1) / 2.0
    rows = []
    for length in WAVELENGTHS:
        wave = 2.0 * math.pi / length
        for angle in (x0 * ux, (x0 - 1.0) * ux, -2.0 * ux, x0 * ux + y0 * uy, x0 * ux - y0 * uy):
            rows += [np.cos(wave * angle), np.sin(wave * angle)]
        rows += [np.zeros_like(ux)] * 6
    return tiled(np.stack(rows).astype(np.float32))


def make_tables(ny, cy):
    _, uy = angles()
    k = np.arange(ny // 2)
    group, lane = k // 128, k % 128
    y = (group * 4 + (lane % 32) // 8) * cy + (lane // 32) * 8 + lane % 8
    v = (ny - 1) / 2.0 - y
    rows = []
    for length in WAVELENGTHS:
        phase = (2.0 * math.pi / length) * v[:, None] * uy[None, :]
        for table in (np.cos(phase), np.sin(phase)):
            high = table.astype(np.float32).astype(BF16)
            rows += [high, (table - high.astype(np.float64)).astype(np.float32).astype(BF16)]
    return tiled(np.concatenate(rows))


def far_kernel(
    ngx, ngy, nx, ny, g_ref, seeds, tables, e_in, h_in, p_in, far, e_out, h_out, p_out,
    a_high, a_low, e_pass, h_pass, p_pass, sem,
):
    pid = pl.program_id(0)
    half = 2 * nx
    depth = ny // 2
    fields = enumerate(zip((e_in, h_in, p_in), (e_pass, h_pass, p_pass), (e_out, h_out, p_out)))
    moves = [
        (pltpu.make_async_copy(src, mid, sem.at[0, i]), pltpu.make_async_copy(mid, dst, sem.at[1, i]))
        for i, (src, mid, dst) in fields
    ]

    @pl.when(pid == 0)
    def _():
        for load, _ in moves:
            load.start()
        quarter = lax.broadcasted_iota(jnp.int32, (32, 128), 1) // 32
        for s in range(2):
            for x in range(ngx // 2):
                for group in range(ngy // 8):
                    kinds = [[], [], [], []]
                    for y in range(4 * group, 4 * group + 4):
                        low_x, high_x = x * ngy, (ngx - 1 - x) * ngy
                        t00, t10 = g_ref[s, low_x + y], g_ref[s, high_x + y]
                        t01, t11 = g_ref[s, low_x + ngy - 1 - y], g_ref[s, high_x + ngy - 1 - y]
                        even0, even1, odd0, odd1 = t10 + t00, t11 + t01, t10 - t00, t11 - t01
                        for kind, tile in zip(kinds, (even0 + even1, odd0 + odd1, even1 - even0, odd1 - odd0)):
                            kind.append(tile)
                    turned = jnp.concatenate(kinds[0] + kinds[1] + kinds[2] + kinds[3], axis=0).T
                    for kind in range(4):
                        block = jnp.zeros((32, 128), F32)
                        for yb in range(4):
                            piece = turned[32 * yb : 32 * yb + 32, :]
                            shift = (32 * (yb - kind)) % 128
                            if shift:
                                piece = pltpu.roll(piece, shift, 1)
                            block = jnp.where(quarter == yb, piece, block)
                        high = block.astype(BF16)
                        rows = pl.ds((2 * s + kind % 2) * half + 32 * x, 32)
                        lanes = pl.ds(128 * group, 128)
                        a_high[kind // 2, rows, lanes] = high
                        a_low[kind // 2, rows, lanes] = (block - high.astype(F32)).astype(BF16)

    @pl.when(pid == 1)
    def _():
        for load, save in moves:
            load.wait()
            save.start()

    scale = 1.0 / math.sqrt(nx * ny)
    sub = lax.broadcasted_iota(jnp.int32, (8, PART), 0)
    top = sub < 4
    lane = lax.broadcasted_iota(jnp.int32, (8, 128), 1)
    first = lane < 64
    mirror = 127 - lane

    def times(a, b):
        return (a[0] * b[0] - a[1] * b[1], a[0] * b[1] + a[1] * b[0])

    for o in range(0, TILE, PART):
        lanes = slice(o, o + PART)
        for f in range(2):
            omega = 2.0 * math.pi / WAVELENGTHS[f]
            kappa = [math.cos(omega * (s + 1) * DT) * scale for s in range(2)]
            sigma = [math.sin(omega * (s + 1) * DT) * scale for s in range(2)]

            def seed(i):
                row = 16 * f + i
                return jnp.broadcast_to(seeds[0, row : row + 1, lanes], (8, PART))

            sums = []
            for trig in range(2):
                at = (2 * f + trig) * 2 * depth
                high = tables[0, at : at + depth, lanes]
                low = tables[0, at + depth : at + 2 * depth, lanes]
                ah, al = a_high[trig], a_low[trig]
                sums.append(jnp.dot(
                    jnp.concatenate([ah, ah, al], axis=1), jnp.concatenate([high, low, high], axis=0),
                    preferred_element_type=F32))
            w = (jnp.where(top, seed(0), seed(2)), jnp.where(top, seed(1), seed(3)))
            e2 = (seed(4), seed(5))
            acc = [[None] * 4, [None] * 4]
            for g in range(nx // 4):
                for s in range(2):
                    for trig in range(2):
                        for odd in range(2):
                            at = (2 * s + odd) * half + 8 * g
                            term = sums[trig][at : at + 8, :] * w[odd]
                            i = 2 * trig + odd
                            acc[s][i] = term if g == 0 else acc[s][i] + term
                if g + 1 < nx // 4:
                    w = times(w, e2)
            ck, sk, dk, rk = [acc[0][i] * kappa[0] + acc[1][i] * kappa[1] for i in range(4)]
            cg, sg, dg, rg = [acc[0][i] * sigma[0] + acc[1][i] * sigma[1] for i in range(4)]
            re_same, re_diff = ck - rk, ck + rk
            im_same, im_diff = cg - rg, cg + rg
            plus_k, minus_k = sk + dk, sk - dk
            plus_g, minus_g = sg + dg, sg - dg
            quads = (
                (re_same + plus_g, plus_k - im_same),
                (re_diff - minus_g, -minus_k - im_diff),
                (re_same - plus_g, -plus_k - im_same),
                (re_diff + minus_g, minus_k - im_diff),
            )
            same = (seed(6), jnp.where(top, -seed(7), seed(7)))
            diff = (seed(8), jnp.where(top, -seed(9), seed(9)))
            done = []
            for q, (re, im) in enumerate(quads):
                both = jnp.where(top, re, im) + pltpu.roll(jnp.where(top, im, re), 4, 0)
                turn = (same, diff)[q % 2]
                swing = pltpu.roll(both, 4, 0) * turn[1]
                done.append(both * turn[0] + (swing if q in (0, 3) else -swing))
            for pair in range(PART // 128):
                cut = slice(128 * pair, 128 * pair + 128)
                for h in range(2):
                    here, back = done[2 * h][:, cut], jnp.take_along_axis(done[2 * h + 1][:, cut], mirror, axis=1)
                    both = (jnp.where(first, here, back), pltpu.roll(jnp.where(first, back, here), 64, 1))
                    for t in range(2):
                        d = (2 * (o // 128 + pair) + t) * 256 + h * 128
                        far[f, 0, :, d : d + 128] = both[t][0:4]
                        far[f, 1, :, d : d + 128] = both[t][4:8]

    @pl.when(pid == pl.num_programs(0) - 1)
    def _():
        for _, save in moves:
            save.wait()


def shards(
    e_field, h_field, polar, polar_prev, material,
    eps_table, delta_table, omega_table, damping_table, surface_flags,
):
    _, cx, cy, nz = e_field.shape
    ngx, ngy = lax.axis_size("gx"), lax.axis_size("gy")
    nx, ny = ngx * cx, ngy * cy
    width = 4 * nx
    hbm = pl.BlockSpec(memory_space=pl.ANY)
    field = jax.ShapeDtypeStruct(e_field.shape, F32)
    dma = pltpu.SemaphoreType.DMA
    e, h, p, g = pl.pallas_call(
        functools.partial(step_kernel, ngx, ngy, eps_table.shape[0]),
        out_shape=(field, field, field, jax.ShapeDtypeStruct((2, ngx * ngy, 8, 128), F32)),
        in_specs=[hbm] * 10,
        out_specs=(hbm,) * 4,
        scratch_shapes=[
            pltpu.VMEM((3, cx + 1, cy, nz), F32),
            pltpu.VMEM((3, cx + 1, cy, nz), F32),
            pltpu.VMEM((3, cx, cy, nz), F32),
            pltpu.VMEM((3, cx, cy, nz), F32),
            pltpu.VMEM((cx, cy, nz), jnp.int32),
            pltpu.VMEM((4, 2, cx, nz), F32),
            pltpu.VMEM((2, 2, cx, nz), F32),
            pltpu.VMEM((2, 2, cx, nz), F32),
            pltpu.VMEM((2, 8, 128), F32),
            *[pltpu.SMEM(table.shape, F32) for table in (eps_table, delta_table, omega_table, damping_table)],
            pltpu.SMEM(surface_flags.shape, jnp.int32),
            dma((10,)), dma((5,)), dma((4, 2 * (cy // BY))), dma((4, 2 * (cy // BY))), dma((4,)), dma((4,)),
            dma((2, ngx * ngy)), dma((2, ngx * ngy)), pltpu.SemaphoreType.REGULAR,
        ],
        compiler_params=pltpu.CompilerParams(
            collective_id=0, has_side_effects=True, vmem_limit_bytes=58 * 1024 * 1024),
    )(e_field, h_field, polar, polar_prev, material,
      eps_table, delta_table, omega_table, damping_table, surface_flags)

    steps = (NDIR // 4) // TILE
    seeds, tables = make_seeds(nx, ny), make_tables(ny, cy)
    far, e, h, p = pl.pallas_call(
        functools.partial(far_kernel, ngx, ngy, nx, ny),
        grid=(steps,),
        out_shape=(jax.ShapeDtypeStruct((2, 2, 4, NDIR), F32), field, field, field),
        in_specs=[
            pl.BlockSpec(g.shape, lambda i: (0, 0, 0, 0)),
            pl.BlockSpec((1, *seeds.shape[1:]), lambda i: (i, 0, 0)),
            pl.BlockSpec((1, *tables.shape[1:]), lambda i: (i, 0, 0)),
            hbm, hbm, hbm,
        ],
        out_specs=(pl.BlockSpec((2, 2, 4, 4 * TILE), lambda i: (0, 0, 0, i)), hbm, hbm, hbm),
        scratch_shapes=[
            pltpu.VMEM((2, 2 * width, ny // 2), BF16),
            pltpu.VMEM((2, 2 * width, ny // 2), BF16),
            *[pltpu.VMEM(e_field.shape, F32)] * 3,
            dma((2, 3)),
        ],
        compiler_params=pltpu.CompilerParams(vmem_limit_bytes=56 * 1024 * 1024),
    )(g, jnp.asarray(seeds), jnp.asarray(tables), e, h, p)
    return e, h, p, far


def solution(mesh):
    cells = P(None, "gx", "gy", None)
    placed = (cells, cells, cells, cells, P("gx", "gy", None), P(), P(), P(), P(), P("gx", "gy"))
    return jax.shard_map(
        shards, mesh=mesh, in_specs=placed, out_specs=(cells, cells, cells, P()), check_vma=False,
    )
```

```python
import functools
import math

import jax
import jax.numpy as jnp
import numpy as np
from jax import lax
from jax.experimental import pallas as pl
from jax.experimental.pallas import tpu as pltpu
from jax.sharding import PartitionSpec as P

NTH = 64
NPH = 256
NDIR = 16384
ZS = 384
DT = 0.55
WAVELENGTHS = (5.0, 4.0)
MESH = pl.DeviceIdType.MESH
F32 = jnp.float32
BF16 = jnp.bfloat16
BY = 8


def coefficients(nmat, nz, eps, delta, omega, damping):
    coef = []
    for m in range(nmat):
        half = jnp.full((1, nz), damping[m], F32) * (DT / 2.0)
        denom = 1.0 + half
        om = jnp.full((1, nz), omega[m], F32)
        square = om * om * (DT * DT)
        coef.append((
            (2.0 - square) / denom,
            (half - 1.0) / denom,
            jnp.full((1, nz), delta[m], F32) * square / denom,
            1.0 / jnp.full((1, nz), eps[m], F32),
        ))
    return coef


def step_kernel(
    ngx, ngy, nmat,
    e_in, h_in, p_in, q_in, m_in, eps_in, delta_in, omega_in, damping_in, flags_in,
    e_out, h_out, p_out, g_out,
    E, H, PA, PB, MAT, xstage, ystage, cstage, xe, xh, ye, yh, ce, G, eps, delta, omega, damping, flags,
    in_sem, out_sem, xs_sem, xr_sem, ys_sem, yr_sem, cs_sem, cr_sem, g1s, g1r, all_in,
):
    cx, cy, nz = MAT.shape
    gx = lax.axis_index("gx")
    gy = lax.axis_index("gy")

    loads = [
        pltpu.make_async_copy(e_in, E, in_sem.at[0]),
        pltpu.make_async_copy(h_in, H, in_sem.at[1]),
        pltpu.make_async_copy(p_in, PA, in_sem.at[2]),
        pltpu.make_async_copy(q_in, PB, in_sem.at[3]),
        pltpu.make_async_copy(m_in, MAT, in_sem.at[4]),
        pltpu.make_async_copy(eps_in, eps, in_sem.at[5]),
        pltpu.make_async_copy(delta_in, delta, in_sem.at[6]),
        pltpu.make_async_copy(omega_in, omega, in_sem.at[7]),
        pltpu.make_async_copy(damping_in, damping, in_sem.at[8]),
        pltpu.make_async_copy(flags_in, flags, in_sem.at[9]),
    ]
    for load in loads:
        load.start()

    barrier = pltpu.get_barrier_semaphore()
    for k in range(1, ngx):
        pl.semaphore_signal(barrier, inc=1, device_id=(lax.rem(gx + k, ngx), gy), device_id_type=MESH)
    for k in range(1, ngy):
        pl.semaphore_signal(barrier, inc=1, device_id=(gx, lax.rem(gy + k, ngy)), device_id_type=MESH)

    for dx, dy in ((1, ngy - 1), (ngx - 1, 1)):
        pl.semaphore_signal(
            barrier, inc=1, device_id=(lax.rem(gx + dx, ngx), lax.rem(gy + dy, ngy)), device_id_type=MESH)

    not_low_x, not_high_x = gx > 0, gx < ngx - 1
    not_low_y, not_high_y = gy > 0, gy < ngy - 1
    dt_x = jnp.where(not_low_x, DT, 0.0)
    dt_y = jnp.where(not_low_y, DT, 0.0)

    def clear(ref):
        ref[...] = jnp.zeros(ref.shape, F32)

    pl.when(gx == ngx - 1)(lambda: clear(xe))
    pl.when(gx == 0)(lambda: clear(xh))
    pl.when(gy == ngy - 1)(lambda: clear(ye))
    pl.when(gy == 0)(lambda: clear(yh))
    for kind, there in ((0, not_low_x & not_high_y), (1, not_high_x & not_low_y)):

        @pl.when(jnp.logical_not(there))
        def _():
            for step in range(2):
                ce[step, kind] = jnp.zeros((1, nz), F32)

    sends_x, takes_x = (not_low_x, not_high_x), (not_high_x, not_low_x)
    sends_y, takes_y = (not_low_y, not_high_y), (not_high_y, not_low_y)

    def x_copies(step, way, block):
        copies = []
        for i in range(2):
            rows = pl.ds(block * BY, BY)
            src = E.at[1 + i, 0, rows] if way == 0 else xstage.at[step, i, rows]
            dst = (xe, xh)[way].at[step, i, rows]
            sem = 2 * block + i
            copies.append(pltpu.make_async_remote_copy(
                src_ref=src, dst_ref=dst, send_sem=xs_sem.at[step, way, sem], recv_sem=xr_sem.at[step, way, sem],
                device_id=(lax.rem(gx + (ngx - 1, 1)[way], ngx), gy), device_id_type=MESH))
        return copies

    def y_copy(step, way):
        return pltpu.make_async_remote_copy(
            src_ref=ystage.at[step, way], dst_ref=(ye, yh)[way].at[step],
            send_sem=ys_sem.at[step, way], recv_sem=yr_sem.at[step, way],
            device_id=(gx, lax.rem(gy + (ngy - 1, 1)[way], ngy)), device_id_type=MESH)

    sends_c = (not_high_x & not_low_y, not_low_x & not_high_y)
    takes_c = (not_low_x & not_high_y, not_high_x & not_low_y)

    def c_copy(step, kind):
        dx, dy = ((1, ngy - 1), (ngx - 1, 1))[kind]
        return pltpu.make_async_remote_copy(
            src_ref=cstage.at[step, kind], dst_ref=ce.at[step, kind],
            send_sem=cs_sem.at[step, kind], recv_sem=cr_sem.at[step, kind],
            device_id=(lax.rem(gx + dx, ngx), lax.rem(gy + dy, ngy)), device_id_type=MESH)

    def send_x(step, way, block):
        @pl.when(sends_x[way])
        def _():
            for copy in x_copies(step, way, block):
                copy.start()

    def take_x(step, way, block):
        @pl.when(takes_x[way])
        def _():
            for copy in x_copies(step, way, block):
                copy.wait_recv()

    def sent_x(step, way):
        @pl.when(sends_x[way])
        def _():
            for block in blocks:
                for copy in x_copies(step, way, block):
                    copy.wait_send()

    def send_y(step, way):
        pl.when(sends_y[way])(lambda: y_copy(step, way).start())

    def take_y(step, way):
        pl.when(takes_y[way])(lambda: y_copy(step, way).wait_recv())

    def sent_y(step, way):
        pl.when(sends_y[way])(lambda: y_copy(step, way).wait_send())

    def send_c(step, kind):
        if kind == 0:
            cstage[step, 0] = E[0, cx - 1, 0:1, :]
        else:
            cstage[step, 1] = E[1, 0, cy - 1 : cy, :]
        pl.when(sends_c[kind])(lambda: c_copy(step, kind).start())

    def take_c(step, kind):
        pl.when(takes_c[kind])(lambda: c_copy(step, kind).wait_recv())

    def sent_c(step, kind):
        pl.when(sends_c[kind])(lambda: c_copy(step, kind).wait_send())

    blocks = range(cy // BY)
    last = cy // BY - 1

    row_id = lax.broadcasted_iota(jnp.int32, (BY, nz), 0)
    lane_id = lax.broadcasted_iota(jnp.int32, (BY, nz), 1)

    def up_y(v, row):
        return jnp.where(row_id == BY - 1, row, pltpu.roll(v, BY - 1, 0))

    def up_z(v):
        return jnp.where(lane_id == nz - 1, 0.0, pltpu.roll(v, nz - 1, 1))

    def down_y(v, row):
        return jnp.where(row_id == 0, row, pltpu.roll(v, 1, 0))

    def down_z(v):
        return jnp.where(lane_id == 0, 0.0, pltpu.roll(v, 1, 1))

    def part_x(step, block):
        here, x, y = pl.ds(block * BY, BY), cx - 1, block * BY
        ex, ey, ez = E[0, x, here, :], E[1, x, here, :], E[2, x, here, :]
        rx = E[0, x, y + BY : y + BY + 1, :] if block < last else jnp.zeros((1, nz), F32)
        xstage[step, 0, here, :] = H[1, x, here, :] - DT * ((up_z(ex) - ex) + ez)
        xstage[step, 1, here, :] = H[2, x, here, :] + DT * (ey + (up_y(ex, rx) - ex))
        send_x(step, 1, block)

    def part_y(step):
        here = pl.ds(cy - BY, BY)
        for x in range(cx):
            ex, ey, ez = E[0, x, here, :], E[1, x, here, :], E[2, x, here, :]
            slope = E[1, x + 1, here, :] - ey if x < cx - 1 else -ey
            part_hx = H[0, x, here, :] + DT * (ez + (up_z(ey) - ey))
            part_hz = H[2, x, here, :] - DT * (slope + ex)
            ystage[step, 1, 0, x : x + 1, :] = part_hx[BY - 1 : BY, :]
            ystage[step, 1, 1, x : x + 1, :] = part_hz[BY - 1 : BY, :]
        send_y(step, 1)

    def rows_y(step):
        for i, c in enumerate((0, 2)):
            for x in range(cx):
                ystage[step, 0, i, x : x + 1, :] = E[c, x, 0:1, :]
        send_y(step, 0)

    def h_plane(step, x, blocks):
        for y in [BY * block for block in blocks]:
            here = pl.ds(y, BY)
            ex, ey, ez = E[0, x, here, :], E[1, x, here, :], E[2, x, here, :]
            if y + BY < cy:
                rx, rz = E[0, x, y + BY : y + BY + 1, :], E[2, x, y + BY : y + BY + 1, :]
            else:
                rx, rz = ye[step, 0, pl.ds(x, 1), :], ye[step, 1, pl.ds(x, 1), :]
            if isinstance(x, int) and x == cx - 1:
                eyx, ezx = xe[step, 0, here, :], xe[step, 1, here, :]
            else:
                eyx, ezx = E[1, x + 1, here, :], E[2, x + 1, here, :]
            curl_x = (up_y(ez, rz) - ez) - (up_z(ey) - ey)
            curl_y = (up_z(ex) - ex) - (ezx - ez)
            curl_z = (eyx - ey) - (up_y(ex, rx) - ex)
            H[0, x, here, :] = H[0, x, here, :] - DT * curl_x
            H[1, x, here, :] = H[1, x, here, :] - DT * curl_y
            H[2, x, here, :] = H[2, x, here, :] - DT * curl_z

    def e_plane(step, x, coef, blocks):
        now, old = (PA, PB) if step == 0 else (PB, PA)
        fixed = isinstance(x, int)
        for y in [BY * block for block in blocks]:
            here = pl.ds(y, BY)
            mat = MAT[x, here, :]
            vox = [jnp.broadcast_to(coef[nmat - 1][i], (BY, nz)) for i in range(4)]
            for m in range(nmat - 1):
                hit = mat == m
                vox = [jnp.where(hit, coef[m][i], vox[i]) for i in range(4)]
            a, b, c, inv = vox
            hx, hy, hz = H[0, x, here, :], H[1, x, here, :], H[2, x, here, :]
            if y > 0:
                rx, rz = H[0, x, y - 1 : y, :], H[2, x, y - 1 : y, :]
            else:
                rx = yh[step, 0, pl.ds(x, 1), :] - dt_y * E[2, x, 0:1, :]
                edge = E[0, x, 0:1, :]
                if fixed and x == cx - 1:
                    edge = edge - ce[step, 1]
                rz = yh[step, 1, pl.ds(x, 1), :] + dt_y * edge
            if fixed and x == 0:
                hyx = xh[step, 0, here, :] + dt_x * E[2, 0, here, :]
                edge = E[1, 0, here, :]
                if y + BY == cy:
                    edge = jnp.where(row_id == BY - 1, edge - ce[step, 0], edge)
                hzx = xh[step, 1, here, :] - dt_x * edge
            else:
                hyx, hzx = H[1, x - 1, here, :], H[2, x - 1, here, :]
            curls = (
                (hz - down_y(hz, rz)) - (hy - down_z(hy)),
                (hx - down_z(hx)) - (hz - hzx),
                (hy - hyx) - (hx - down_y(hx, rx)),
            )
            for i in range(3):
                e, p = E[i, x, here, :], now[i, x, here, :]
                new = a * p + b * old[i, x, here, :] + c * e
                E[i, x, here, :] = e + (DT * curls[i] - (new - p)) * inv
                old[i, x, here, :] = new

    me = gx * ngy + gy
    count = ngx * ngy
    turn_x, turn_y = 2 * gx >= ngx, 2 * gy >= ngy
    tile_lane = lax.broadcasted_iota(jnp.int32, (8, 128), 1)
    tile_row = lax.broadcasted_iota(jnp.int32, (8, 128), 0)

    def surface(step, flag):
        def body(x, acc):
            at = jnp.where(turn_x, cx - 1 - x, x) * 4
            for yb in range(cy // 8):
                base = jnp.where(turn_y, cy // 8 - 1 - yb, yb) * (4 * cx) + at
                rows = slice(8 * yb, 8 * yb + 8)
                cols = (
                    -H[1, x, rows, ZS : ZS + 1], H[0, x, rows, ZS : ZS + 1],
                    E[1, x, rows, ZS : ZS + 1], -E[0, x, rows, ZS : ZS + 1],
                )
                for j in range(4):
                    acc = jnp.where(tile_lane == base + j, cols[j], acc)
            return acc

        tile = lax.fori_loop(0, cx, body, jnp.zeros((8, 128), F32)) * flag
        back = tile
        for bit in (1, 2, 4):
            back = jnp.where((tile_row & bit) != 0, pltpu.roll(back, bit, 0), pltpu.roll(back, 8 - bit, 0))
        G[step] = jnp.where(turn_y, back, tile)

    def peer(step, k):
        to = lax.rem(me + k, count)
        return pltpu.make_async_remote_copy(
            src_ref=G.at[step], dst_ref=g_out.at[step, me], send_sem=g1s.at[step, k], recv_sem=g1r.at[step, k],
            device_id=(to // ngy, lax.rem(to, ngy)), device_id_type=MESH)

    def own(step):
        return pltpu.make_async_copy(G.at[step], g_out.at[step, me], out_sem.at[3 + step])

    def gather_start(step):
        own(step).start()

        @pl.loop(1, count)
        def _(k):
            peer(step, k).start()

    def gather_end(step):
        own(step).wait()

        @pl.loop(1, count)
        def _(k):
            peer(step, k).wait()

    loads[0].wait()
    pl.semaphore_wait(barrier, ngx + ngy)
    send_c(0, 0)
    send_c(0, 1)
    for block in blocks:
        send_x(0, 0, block)
    rows_y(0)
    loads[1].wait()
    for block in blocks:
        part_x(0, block)
    part_y(0)
    for k in range(1, ngy):
        pl.semaphore_signal(all_in, inc=1, device_id=(gx, lax.rem(gy + k, ngy)), device_id_type=MESH)
    for load in loads[5:]:
        load.wait()

    coef = coefficients(nmat, nz, eps, delta, omega, damping)
    flag = flags[0, 0].astype(F32)

    for step in range(2):

        @pl.loop(0, cx - 1)
        def _(x):
            h_plane(step, x, range(last))

        if step == 0:
            for load in loads[2:5]:
                load.wait()
        else:
            gather_start(0)

        @pl.loop(1, cx - 1)
        def _(x):
            e_plane(step, x, coef, range(1, last))

        for block in range(last):
            take_x(step, 0, block)
            h_plane(step, cx - 1, [block])
        take_y(step, 0)
        take_x(step, 0, last)
        h_plane(step, cx - 1, [last])

        @pl.loop(0, cx - 1)
        def _(x):
            h_plane(step, x, [last])

        if step == 1:
            pltpu.make_async_copy(H, h_out, out_sem.at[0]).start()
        sent_x(step, 0)
        take_y(step, 1)
        take_c(step, 1)
        for block in range(last, -1, -1):
            e_plane(step, cx - 1, coef, [block])
            if step == 0:
                part_x(1, block)
        if step == 0:
            send_c(1, 0)
        for block in blocks:
            take_x(step, 1, block)
            if block == last:
                take_c(step, 0)
            e_plane(step, 0, coef, [block])
            if step == 0:
                send_x(1, 0, block)
        if step == 0:
            send_c(1, 1)

        @pl.loop(1, cx - 1)
        def _(x):
            e_plane(step, x, coef, [0, last])

        if step == 0:
            rows_y(1)
            part_y(1)
        surface(step, flag)
        if step == 0:
            pl.semaphore_wait(all_in, ngy - 1)
        else:
            gather_start(1)

    saves = [
        pltpu.make_async_copy(H, h_out, out_sem.at[0]),
        pltpu.make_async_copy(E, e_out, out_sem.at[1]),
        pltpu.make_async_copy(PA, p_out, out_sem.at[2]),
    ]
    saves[1].start()
    saves[2].start()
    for step in range(2):
        sent_x(step, 1)
        for i in range(2):
            sent_y(step, i)
            sent_c(step, i)
    gather_end(0)
    gather_end(1)
    for save in saves:
        save.wait()


TILE = 1024
PART = 256


def angles():
    theta = (np.arange(NTH, dtype=np.float64)[:, None] + 0.5) * (math.pi / 2.0 / NTH)
    phi = (np.arange(NPH // 4, dtype=np.float64)[None, :] + 0.5) * (2.0 * math.pi / NPH)
    ux = (np.sin(theta) * np.cos(phi)).reshape(-1)
    uy = (np.sin(theta) * np.sin(phi)).reshape(-1)
    return ux, uy


def tiled(rows):
    return np.ascontiguousarray(rows.reshape(rows.shape[0], -1, TILE).swapaxes(0, 1))


def make_seeds(nx, ny):
    ux, uy = angles()
    x0, y0 = (nx - 1) / 2.0, (ny - 1) / 2.0
    rows = []
    for length in WAVELENGTHS:
        wave = 2.0 * math.pi / length
        turns = [(y0 - y) * uy for y in range(8)]
        rows += [np.cos(wave * angle) for angle in turns] + [np.sin(wave * angle) for angle in turns]
        for angle in (x0 * ux, (x0 - 1.0) * ux, -2.0 * ux, x0 * ux + y0 * uy, x0 * ux - y0 * uy, -8.0 * uy, -16.0 * uy):
            rows += [np.cos(wave * angle), np.sin(wave * angle)]
        rows += [np.zeros_like(ux)] * 2
    return tiled(np.stack(rows).astype(np.float32))


def far_kernel(
    ngx, ngy, nx, ny, g_ref, seeds, e_in, h_in, p_in, far, e_out, h_out, p_out,
    a_high, a_low, e_pass, h_pass, p_pass, sem,
):
    pid = pl.program_id(0)
    half = 2 * nx
    depth = ny // 2
    per = ny // ngy // 8
    fields = enumerate(zip((e_in, h_in, p_in), (e_pass, h_pass, p_pass), (e_out, h_out, p_out)))
    moves = [
        (pltpu.make_async_copy(src, mid, sem.at[0, i]), pltpu.make_async_copy(mid, dst, sem.at[1, i]))
        for i, (src, mid, dst) in fields
    ]

    @pl.when(pid == 0)
    def _():
        for load, _ in moves:
            load.start()
        quarter = lax.broadcasted_iota(jnp.int32, (32, 128), 1) // 32
        for s in range(2):
            for x in range(ngx // 2):
                for group in range(ngy // 8):
                    kinds = [[], [], [], []]
                    for y in range(4 * group, 4 * group + 4):
                        low_x, high_x = x * ngy, (ngx - 1 - x) * ngy
                        t00, t10 = g_ref[s, low_x + y], g_ref[s, high_x + y]
                        t01, t11 = g_ref[s, low_x + ngy - 1 - y], g_ref[s, high_x + ngy - 1 - y]
                        even0, even1, odd0, odd1 = t10 + t00, t11 + t01, t10 - t00, t11 - t01
                        for kind, tile in zip(kinds, (even0 + even1, odd0 + odd1, even1 - even0, odd1 - odd0)):
                            kind.append(tile)
                    turned = jnp.concatenate(kinds[0] + kinds[1] + kinds[2] + kinds[3], axis=0).T
                    for kind in range(4):
                        block = jnp.zeros((32, 128), F32)
                        for yb in range(4):
                            piece = turned[32 * yb : 32 * yb + 32, :]
                            shift = (32 * (yb - kind)) % 128
                            if shift:
                                piece = pltpu.roll(piece, shift, 1)
                            block = jnp.where(quarter == yb, piece, block)
                        high = block.astype(BF16)
                        rows = pl.ds((2 * s + kind % 2) * half + 32 * x, 32)
                        lanes = pl.ds(128 * group, 128)
                        a_high[kind // 2, rows, lanes] = high
                        a_low[kind // 2, rows, lanes] = (block - high.astype(F32)).astype(BF16)

    @pl.when(pid == 1)
    def _():
        for load, save in moves:
            load.wait()
            save.start()

    scale = 1.0 / math.sqrt(nx * ny)
    sub = lax.broadcasted_iota(jnp.int32, (8, PART), 0)
    top = sub < 4
    lane = lax.broadcasted_iota(jnp.int32, (8, 128), 1)
    first = lane < 64
    mirror = 127 - lane

    def times(a, b):
        return (a[0] * b[0] - a[1] * b[1], a[0] * b[1] + a[1] * b[0])

    for o in range(0, TILE, PART):
        lanes = slice(o, o + PART)
        for f in range(2):
            omega = 2.0 * math.pi / WAVELENGTHS[f]
            kappa = [math.cos(omega * (s + 1) * DT) * scale for s in range(2)]
            sigma = [math.sin(omega * (s + 1) * DT) * scale for s in range(2)]

            def seed(i):
                row = 32 * f + 16 + i
                return jnp.broadcast_to(seeds[0, row : row + 1, lanes], (8, PART))

            v = (seeds[0, 32 * f : 32 * f + 8, lanes], seeds[0, 32 * f + 8 : 32 * f + 16, lanes])
            e16 = (seed(12), seed(13))
            w = times(v, (seed(10), seed(11)))
            waves = []
            for j in range(depth // 16):
                waves += [v, w]
                if 16 * (j + 1) < depth:
                    v, w = times(v, e16), times(w, e16)
            order = [
                (4 * group + y) * per + yb for group in range(depth // 128) for yb in range(per) for y in range(4)
            ]
            sums = []
            for trig in range(2):
                full = jnp.concatenate([waves[j][trig] for j in order], axis=0)
                high = full.astype(BF16)
                low = (full - high.astype(F32)).astype(BF16)
                ah, al = a_high[trig], a_low[trig]
                sums.append(jnp.dot(
                    jnp.concatenate([ah, ah, al], axis=1), jnp.concatenate([high, low, high], axis=0),
                    preferred_element_type=F32))
            w = (jnp.where(top, seed(0), seed(2)), jnp.where(top, seed(1), seed(3)))
            e2 = (seed(4), seed(5))
            acc = [[None] * 4, [None] * 4]
            for g in range(nx // 4):
                for s in range(2):
                    for trig in range(2):
                        for odd in range(2):
                            at = (2 * s + odd) * half + 8 * g
                            term = sums[trig][at : at + 8, :] * w[odd]
                            i = 2 * trig + odd
                            acc[s][i] = term if g == 0 else acc[s][i] + term
                if g + 1 < nx // 4:
                    w = times(w, e2)
            ck, sk, dk, rk = [acc[0][i] * kappa[0] + acc[1][i] * kappa[1] for i in range(4)]
            cg, sg, dg, rg = [acc[0][i] * sigma[0] + acc[1][i] * sigma[1] for i in range(4)]
            re_same, re_diff = ck - rk, ck + rk
            im_same, im_diff = cg - rg, cg + rg
            plus_k, minus_k = sk + dk, sk - dk
            plus_g, minus_g = sg + dg, sg - dg
            quads = (
                (re_same + plus_g, plus_k - im_same),
                (re_diff - minus_g, -minus_k - im_diff),
                (re_same - plus_g, -plus_k - im_same),
                (re_diff + minus_g, minus_k - im_diff),
            )
            same = (seed(6), jnp.where(top, -seed(7), seed(7)))
            diff = (seed(8), jnp.where(top, -seed(9), seed(9)))
            done = []
            for q, (re, im) in enumerate(quads):
                both = jnp.where(top, re, im) + pltpu.roll(jnp.where(top, im, re), 4, 0)
                turn = (same, diff)[q % 2]
                swing = pltpu.roll(both, 4, 0) * turn[1]
                done.append(both * turn[0] + (swing if q in (0, 3) else -swing))
            for pair in range(PART // 128):
                cut = slice(128 * pair, 128 * pair + 128)
                for h in range(2):
                    here, back = done[2 * h][:, cut], jnp.take_along_axis(done[2 * h + 1][:, cut], mirror, axis=1)
                    both = (jnp.where(first, here, back), pltpu.roll(jnp.where(first, back, here), 64, 1))
                    for t in range(2):
                        d = (2 * (o // 128 + pair) + t) * 256 + h * 128
                        far[f, 0, :, d : d + 128] = both[t][0:4]
                        far[f, 1, :, d : d + 128] = both[t][4:8]

    @pl.when(pid == pl.num_programs(0) - 1)
    def _():
        for _, save in moves:
            save.wait()


def shards(
    e_field, h_field, polar, polar_prev, material,
    eps_table, delta_table, omega_table, damping_table, surface_flags,
):
    _, cx, cy, nz = e_field.shape
    ngx, ngy = lax.axis_size("gx"), lax.axis_size("gy")
    nx, ny = ngx * cx, ngy * cy
    width = 4 * nx
    hbm = pl.BlockSpec(memory_space=pl.ANY)
    field = jax.ShapeDtypeStruct(e_field.shape, F32)
    dma = pltpu.SemaphoreType.DMA
    e, h, p, g = pl.pallas_call(
        functools.partial(step_kernel, ngx, ngy, eps_table.shape[0]),
        out_shape=(field, field, field, jax.ShapeDtypeStruct((2, ngx * ngy, 8, 128), F32)),
        in_specs=[hbm] * 10,
        out_specs=(hbm,) * 4,
        scratch_shapes=[
            *[pltpu.VMEM(e_field.shape, F32)] * 4,
            pltpu.VMEM((cx, cy, nz), jnp.int32),
            pltpu.VMEM((2, 2, cy, nz), F32),
            pltpu.VMEM((2, 2, 2, cx, nz), F32),
            pltpu.VMEM((2, 2, 1, nz), F32),
            pltpu.VMEM((2, 2, cy, nz), F32),
            pltpu.VMEM((2, 2, cy, nz), F32),
            pltpu.VMEM((2, 2, cx, nz), F32),
            pltpu.VMEM((2, 2, cx, nz), F32),
            pltpu.VMEM((2, 2, 1, nz), F32),
            pltpu.VMEM((2, 8, 128), F32),
            *[pltpu.SMEM(table.shape, F32) for table in (eps_table, delta_table, omega_table, damping_table)],
            pltpu.SMEM(surface_flags.shape, jnp.int32),
            dma((10,)), dma((5,)), *[dma((2, 2, 2 * (cy // BY)))] * 2, *[dma((2, 2))] * 4,
            dma((2, ngx * ngy)), dma((2, ngx * ngy)), pltpu.SemaphoreType.REGULAR,
        ],
        compiler_params=pltpu.CompilerParams(
            collective_id=0, has_side_effects=True, vmem_limit_bytes=58 * 1024 * 1024),
    )(e_field, h_field, polar, polar_prev, material,
      eps_table, delta_table, omega_table, damping_table, surface_flags)

    steps = (NDIR // 4) // TILE
    seeds = make_seeds(nx, ny)
    far, e, h, p = pl.pallas_call(
        functools.partial(far_kernel, ngx, ngy, nx, ny),
        grid=(steps,),
        out_shape=(jax.ShapeDtypeStruct((2, 2, 4, NDIR), F32), field, field, field),
        in_specs=[
            pl.BlockSpec(g.shape, lambda i: (0, 0, 0, 0)),
            pl.BlockSpec((1, *seeds.shape[1:]), lambda i: (i, 0, 0)),
            hbm, hbm, hbm,
        ],
        out_specs=(pl.BlockSpec((2, 2, 4, 4 * TILE), lambda i: (0, 0, 0, i)), hbm, hbm, hbm),
        scratch_shapes=[
            pltpu.VMEM((2, 2 * width, ny // 2), BF16),
            pltpu.VMEM((2, 2 * width, ny // 2), BF16),
            *[pltpu.VMEM(e_field.shape, F32)] * 3,
            dma((2, 3)),
        ],
        compiler_params=pltpu.CompilerParams(vmem_limit_bytes=56 * 1024 * 1024),
    )(g, jnp.asarray(seeds), e, h, p)
    return e, h, p, far


def solution(mesh):
    cells = P(None, "gx", "gy", None)
    placed = (cells, cells, cells, cells, P("gx", "gy", None), P(), P(), P(), P(), P("gx", "gy"))
    return jax.shard_map(
        shards, mesh=mesh, in_specs=placed, out_specs=(cells, cells, cells, P()), check_vma=False,
    )
```

```python
import functools
import math

import jax
import jax.numpy as jnp
import numpy as np
from jax import lax
from jax.experimental import pallas as pl
from jax.experimental.pallas import tpu as pltpu
from jax.sharding import PartitionSpec as P

NTH = 64
NPH = 256
NDIR = 16384
ZS = 384
DT = 0.55
WAVELENGTHS = (5.0, 4.0)
MESH = pl.DeviceIdType.MESH
F32 = jnp.float32
BF16 = jnp.bfloat16
BY = 8
H_PARTS = (((128, 512), (0, 128)), ((256, 512), (0, 256)))
E_PARTS = (((256, 512), (0, 256)), ((384, 512), (0, 384)))


def coefficients(nmat, nz, eps, delta, omega, damping):
    coef = []
    for m in range(nmat):
        half = jnp.full((1, nz), damping[m], F32) * (DT / 2.0)
        denom = 1.0 + half
        om = jnp.full((1, nz), omega[m], F32)
        square = om * om * (DT * DT)
        coef.append((
            (2.0 - square) / denom,
            (half - 1.0) / denom,
            jnp.full((1, nz), delta[m], F32) * square / denom,
            1.0 / jnp.full((1, nz), eps[m], F32),
        ))
    return coef


def step_kernel(
    ngx, ngy, nmat,
    e_in, h_in, p_in, q_in, m_in, eps_in, delta_in, omega_in, damping_in, flags_in,
    e_out, h_out, p_out, g_out,
    E, H, PA, PB, MAT, xstage, ystage, cstage, xe, xh, ye, yh, ce, G, eps, delta, omega, damping, flags,
    in_sem, out_sem, xs_sem, xr_sem, ys_sem, yr_sem, cs_sem, cr_sem, g1s, g1r, all_in,
):
    cx, cy, nz = MAT.shape
    gx = lax.axis_index("gx")
    gy = lax.axis_index("gy")

    loads = [
        pltpu.make_async_copy(e_in, E, in_sem.at[0]),
        pltpu.make_async_copy(h_in, H, in_sem.at[1]),
        pltpu.make_async_copy(p_in, PA, in_sem.at[2]),
        pltpu.make_async_copy(q_in, PB, in_sem.at[3]),
        pltpu.make_async_copy(m_in, MAT, in_sem.at[4]),
        pltpu.make_async_copy(eps_in, eps, in_sem.at[5]),
        pltpu.make_async_copy(delta_in, delta, in_sem.at[6]),
        pltpu.make_async_copy(omega_in, omega, in_sem.at[7]),
        pltpu.make_async_copy(damping_in, damping, in_sem.at[8]),
        pltpu.make_async_copy(flags_in, flags, in_sem.at[9]),
    ]
    for load in loads[:2] + loads[5:]:
        load.start()

    barrier = pltpu.get_barrier_semaphore()
    for k in range(1, ngx):
        pl.semaphore_signal(barrier, inc=1, device_id=(lax.rem(gx + k, ngx), gy), device_id_type=MESH)
    for k in range(1, ngy):
        pl.semaphore_signal(barrier, inc=1, device_id=(gx, lax.rem(gy + k, ngy)), device_id_type=MESH)

    for dx, dy in ((1, ngy - 1), (ngx - 1, 1)):
        pl.semaphore_signal(
            barrier, inc=1, device_id=(lax.rem(gx + dx, ngx), lax.rem(gy + dy, ngy)), device_id_type=MESH)

    not_low_x, not_high_x = gx > 0, gx < ngx - 1
    not_low_y, not_high_y = gy > 0, gy < ngy - 1
    dt_x = jnp.where(not_low_x, DT, 0.0)
    dt_y = jnp.where(not_low_y, DT, 0.0)

    def clear(ref):
        ref[...] = jnp.zeros(ref.shape, F32)

    pl.when(gx == ngx - 1)(lambda: clear(xe))
    pl.when(gx == 0)(lambda: clear(xh))
    pl.when(gy == ngy - 1)(lambda: clear(ye))
    pl.when(gy == 0)(lambda: clear(yh))
    for kind, there in ((0, not_low_x & not_high_y), (1, not_high_x & not_low_y)):

        @pl.when(jnp.logical_not(there))
        def _():
            for step in range(2):
                ce[step, kind] = jnp.zeros((1, nz), F32)

    sends_x, takes_x = (not_low_x, not_high_x), (not_high_x, not_low_x)
    sends_y, takes_y = (not_low_y, not_high_y), (not_high_y, not_low_y)

    def lanes_of(step, way, part):
        low, high = (H_PARTS, E_PARTS)[way][step][part]
        return pl.ds(low, high - low)

    def x_copies(step, way, part):
        lanes = lanes_of(step, way, part)
        copies = []
        for i in range(2):
            src = E.at[1 + i, 0, :, lanes] if way == 0 else xstage.at[step, i, :, lanes]
            dst = (xe, xh)[way].at[step, i, :, lanes]
            copies.append(pltpu.make_async_remote_copy(
                src_ref=src, dst_ref=dst,
                send_sem=xs_sem.at[step, way, 2 * part + i], recv_sem=xr_sem.at[step, way, 2 * part + i],
                device_id=(lax.rem(gx + (ngx - 1, 1)[way], ngx), gy), device_id_type=MESH))
        return copies

    def y_copy(step, way, part):
        lanes = lanes_of(step, way, part)
        return pltpu.make_async_remote_copy(
            src_ref=ystage.at[step, way, :, :, :, lanes], dst_ref=(ye, yh)[way].at[step, :, :, :, lanes],
            send_sem=ys_sem.at[step, way, part], recv_sem=yr_sem.at[step, way, part],
            device_id=(gx, lax.rem(gy + (ngy - 1, 1)[way], ngy)), device_id_type=MESH)

    sends_c = (not_high_x & not_low_y, not_low_x & not_high_y)
    takes_c = (not_low_x & not_high_y, not_high_x & not_low_y)

    def c_copy(step, kind, part):
        dx, dy = ((1, ngy - 1), (ngx - 1, 1))[kind]
        lanes = lanes_of(step, 1, part)
        return pltpu.make_async_remote_copy(
            src_ref=cstage.at[step, kind, :, lanes], dst_ref=ce.at[step, kind, :, lanes],
            send_sem=cs_sem.at[step, kind, part], recv_sem=cr_sem.at[step, kind, part],
            device_id=(lax.rem(gx + dx, ngx), lax.rem(gy + dy, ngy)), device_id_type=MESH)

    def send_x(step, way, part):
        @pl.when(sends_x[way])
        def _():
            for copy in x_copies(step, way, part):
                copy.start()

    def take_x(step, way, part):
        @pl.when(takes_x[way])
        def _():
            for copy in x_copies(step, way, part):
                copy.wait_recv()

    def sent_x(step, way, part):
        @pl.when(sends_x[way])
        def _():
            for copy in x_copies(step, way, part):
                copy.wait_send()

    def send_y(step, way, part):
        pl.when(sends_y[way])(lambda: y_copy(step, way, part).start())

    def take_y(step, way, part):
        pl.when(takes_y[way])(lambda: y_copy(step, way, part).wait_recv())

    def sent_y(step, way, part):
        pl.when(sends_y[way])(lambda: y_copy(step, way, part).wait_send())

    def send_c(step, part):
        lanes = slice(*E_PARTS[step][part])
        cstage[step, 0, :, lanes] = E[0, cx - 1, 0:1, lanes]
        cstage[step, 1, :, lanes] = E[1, 0, cy - 1 : cy, lanes]
        for kind in range(2):
            pl.when(sends_c[kind])(lambda: c_copy(step, kind, part).start())

    def take_c(step, kind, part):
        pl.when(takes_c[kind])(lambda: c_copy(step, kind, part).wait_recv())

    def sent_c(step, kind, part):
        pl.when(sends_c[kind])(lambda: c_copy(step, kind, part).wait_send())

    blocks = range(cy // BY)
    last = cy // BY - 1

    def ids(span, dim):
        return lax.broadcasted_iota(jnp.int32, (BY, span[1] - span[0]), dim)

    def up_y(v, row, span):
        return jnp.where(ids(span, 0) == BY - 1, row, pltpu.roll(v, BY - 1, 0))

    def down_y(v, row, span):
        return jnp.where(ids(span, 0) == 0, row, pltpu.roll(v, 1, 0))

    def up_z(ref, c, x, here, span):
        low, high = span
        n = high - low
        if high == nz:
            return jnp.where(ids(span, 1) == n - 1, 0.0, pltpu.roll(ref[c, x, here, low:high], n - 1, 1))
        return pltpu.roll(ref[c, x, here, low : high + 128], n + 127, 1)[:, :n]

    def down_z(ref, c, x, here, span):
        low, high = span
        if low == 0:
            return jnp.where(ids(span, 1) == 0, 0.0, pltpu.roll(ref[c, x, here, low:high], 1, 1))
        return pltpu.roll(ref[c, x, here, low - 128 : high], 1, 1)[:, 128:]

    def part_x(step, part):
        span = E_PARTS[step][part]
        lanes, x = slice(*span), cx - 1
        for block in blocks:
            here, y = pl.ds(block * BY, BY), block * BY
            ex, ey, ez = E[0, x, here, lanes], E[1, x, here, lanes], E[2, x, here, lanes]
            rx = E[0, x, y + BY : y + BY + 1, lanes] if block < last else jnp.zeros((1, span[1] - span[0]), F32)
            xstage[step, 0, here, lanes] = H[1, x, here, lanes] - DT * ((up_z(E, 0, x, here, span) - ex) + ez)
            xstage[step, 1, here, lanes] = H[2, x, here, lanes] + DT * (ey + (up_y(ex, rx, span) - ex))
        send_x(step, 1, part)

    def part_y(step, part):
        span = E_PARTS[step][part]
        here, lanes = pl.ds(cy - BY, BY), slice(*span)
        for x in range(cx):
            ex, ey, ez = E[0, x, here, lanes], E[1, x, here, lanes], E[2, x, here, lanes]
            slope = E[1, x + 1, here, lanes] - ey if x < cx - 1 else -ey
            part_hx = H[0, x, here, lanes] + DT * (ez + (up_z(E, 1, x, here, span) - ey))
            part_hz = H[2, x, here, lanes] - DT * (slope + ex)
            ystage[step, 1, 0, x, :, lanes] = part_hx[BY - 1 : BY, :]
            ystage[step, 1, 1, x, :, lanes] = part_hz[BY - 1 : BY, :]
        send_y(step, 1, part)

    def rows_y(step, part):
        lanes = slice(*H_PARTS[step][part])
        for i, c in enumerate((0, 2)):
            for x in range(cx):
                ystage[step, 0, i, x, :, lanes] = E[c, x, 0:1, lanes]
        send_y(step, 0, part)

    def h_plane(step, x, blocks, span):
        lanes = slice(*span)
        for y in [BY * block for block in blocks]:
            here = pl.ds(y, BY)
            ex, ey, ez = E[0, x, here, lanes], E[1, x, here, lanes], E[2, x, here, lanes]
            if y + BY < cy:
                rx, rz = E[0, x, y + BY : y + BY + 1, lanes], E[2, x, y + BY : y + BY + 1, lanes]
            else:
                rx, rz = ye[step, 0, x, :, lanes], ye[step, 1, x, :, lanes]
            if isinstance(x, int) and x == cx - 1:
                eyx, ezx = xe[step, 0, here, lanes], xe[step, 1, here, lanes]
            else:
                eyx, ezx = E[1, x + 1, here, lanes], E[2, x + 1, here, lanes]
            curl_x = (up_y(ez, rz, span) - ez) - (up_z(E, 1, x, here, span) - ey)
            curl_y = (up_z(E, 0, x, here, span) - ex) - (ezx - ez)
            curl_z = (eyx - ey) - (up_y(ex, rx, span) - ex)
            H[0, x, here, lanes] = H[0, x, here, lanes] - DT * curl_x
            H[1, x, here, lanes] = H[1, x, here, lanes] - DT * curl_y
            H[2, x, here, lanes] = H[2, x, here, lanes] - DT * curl_z

    def e_plane(step, x, coef, blocks, span):
        now, old = (PA, PB) if step == 0 else (PB, PA)
        fixed = isinstance(x, int)
        lanes, n = slice(*span), span[1] - span[0]
        for y in [BY * block for block in blocks]:
            here = pl.ds(y, BY)
            mat = MAT[x, here, lanes]
            vox = [jnp.broadcast_to(coef[nmat - 1][i][:, :n], (BY, n)) for i in range(4)]
            for m in range(nmat - 1):
                hit = mat == m
                vox = [jnp.where(hit, coef[m][i][:, :n], vox[i]) for i in range(4)]
            a, b, c, inv = vox
            hx, hy, hz = H[0, x, here, lanes], H[1, x, here, lanes], H[2, x, here, lanes]
            if y > 0:
                rx, rz = H[0, x, y - 1 : y, lanes], H[2, x, y - 1 : y, lanes]
            else:
                rx = yh[step, 0, x, :, lanes] - dt_y * E[2, x, 0:1, lanes]
                edge = E[0, x, 0:1, lanes]
                if fixed and x == cx - 1:
                    edge = edge - ce[step, 1, :, lanes]
                rz = yh[step, 1, x, :, lanes] + dt_y * edge
            if fixed and x == 0:
                hyx = xh[step, 0, here, lanes] + dt_x * E[2, 0, here, lanes]
                edge = E[1, 0, here, lanes]
                if y + BY == cy:
                    edge = jnp.where(ids(span, 0) == BY - 1, edge - ce[step, 0, :, lanes], edge)
                hzx = xh[step, 1, here, lanes] - dt_x * edge
            else:
                hyx, hzx = H[1, x - 1, here, lanes], H[2, x - 1, here, lanes]
            curls = (
                (hz - down_y(hz, rz, span)) - (hy - down_z(H, 1, x, here, span)),
                (hx - down_z(H, 0, x, here, span)) - (hz - hzx),
                (hy - hyx) - (hx - down_y(hx, rx, span)),
            )
            for i in range(3):
                e, p = E[i, x, here, lanes], now[i, x, here, lanes]
                new = a * p + b * old[i, x, here, lanes] + c * e
                E[i, x, here, lanes] = e + (DT * curls[i] - (new - p)) * inv
                old[i, x, here, lanes] = new

    me = gx * ngy + gy
    count = ngx * ngy
    turn_x, turn_y = 2 * gx >= ngx, 2 * gy >= ngy
    tile_lane = lax.broadcasted_iota(jnp.int32, (8, 128), 1)
    tile_row = lax.broadcasted_iota(jnp.int32, (8, 128), 0)

    def surface(step, flag):
        def body(x, acc):
            at = jnp.where(turn_x, cx - 1 - x, x) * 4
            for yb in range(cy // 8):
                base = jnp.where(turn_y, cy // 8 - 1 - yb, yb) * (4 * cx) + at
                rows = slice(8 * yb, 8 * yb + 8)
                cols = (
                    -H[1, x, rows, ZS : ZS + 1], H[0, x, rows, ZS : ZS + 1],
                    E[1, x, rows, ZS : ZS + 1], -E[0, x, rows, ZS : ZS + 1],
                )
                for j in range(4):
                    acc = jnp.where(tile_lane == base + j, cols[j], acc)
            return acc

        tile = lax.fori_loop(0, cx, body, jnp.zeros((8, 128), F32)) * flag
        back = tile
        for bit in (1, 2, 4):
            back = jnp.where((tile_row & bit) != 0, pltpu.roll(back, bit, 0), pltpu.roll(back, 8 - bit, 0))
        G[step] = jnp.where(turn_y, back, tile)

    def peer(step, k):
        to = lax.rem(me + k, count)
        return pltpu.make_async_remote_copy(
            src_ref=G.at[step], dst_ref=g_out.at[step, me], send_sem=g1s.at[step, k], recv_sem=g1r.at[step, k],
            device_id=(to // ngy, lax.rem(to, ngy)), device_id_type=MESH)

    def own(step):
        return pltpu.make_async_copy(G.at[step], g_out.at[step, me], out_sem.at[3 + step])

    def gather_start(step):
        own(step).start()

        @pl.loop(1, count)
        def _(k):
            peer(step, k).start()

    def gather_end(step):
        own(step).wait()

        @pl.loop(1, count)
        def _(k):
            peer(step, k).wait()

    every = (0, nz)
    loads[0].wait()
    pl.semaphore_wait(barrier, ngx + ngy)
    send_c(0, 0)
    send_x(0, 0, 0)
    rows_y(0, 0)
    loads[1].wait()
    for load in loads[2:5]:
        load.start()
    part_x(0, 0)
    part_y(0, 0)
    send_c(0, 1)
    send_x(0, 0, 1)
    rows_y(0, 1)
    part_x(0, 1)
    part_y(0, 1)
    for k in range(1, ngy):
        pl.semaphore_signal(all_in, inc=1, device_id=(gx, lax.rem(gy + k, ngy)), device_id_type=MESH)
    for load in loads[5:]:
        load.wait()

    coef = coefficients(nmat, nz, eps, delta, omega, damping)
    flag = flags[0, 0].astype(F32)

    for step in range(2):

        @pl.loop(0, cx - 1)
        def _(x):
            h_plane(step, x, range(last), every)

        if step == 0:
            for load in loads[2:5]:
                load.wait()
        else:
            gather_start(0)

        @pl.loop(1, cx - 1)
        def _(x):
            e_plane(step, x, coef, range(1, last), every)

        for part in range(2):
            h_span, e_span = H_PARTS[step][part], E_PARTS[step][part]
            take_y(step, 0, part)

            @pl.loop(0, cx - 1)
            def _(x):
                h_plane(step, x, [last], h_span)

            take_x(step, 0, part)
            h_plane(step, cx - 1, blocks, h_span)
            if step == 1 and part == 1:
                pltpu.make_async_copy(H, h_out, out_sem.at[0]).start()
            sent_x(step, 0, part)
            take_y(step, 1, part)
            take_c(step, 1, part)
            e_plane(step, cx - 1, coef, blocks, e_span)
            if step == 0:
                part_x(1, part)
            take_x(step, 1, part)
            take_c(step, 0, part)
            e_plane(step, 0, coef, blocks, e_span)
            if step == 0:
                send_x(1, 0, part)
                send_c(1, part)

            @pl.loop(1, cx - 1)
            def _(x):
                e_plane(step, x, coef, [0, last], e_span)

            if step == 0:
                rows_y(1, part)
                part_y(1, part)
            elif part == 0:
                surface(1, flag)
                gather_start(1)
        if step == 0:
            surface(0, flag)
            pl.semaphore_wait(all_in, ngy - 1)

    saves = [
        pltpu.make_async_copy(H, h_out, out_sem.at[0]),
        pltpu.make_async_copy(E, e_out, out_sem.at[1]),
        pltpu.make_async_copy(PA, p_out, out_sem.at[2]),
    ]
    saves[1].start()
    saves[2].start()
    for step in range(2):
        for part in range(2):
            sent_x(step, 1, part)
            for i in range(2):
                sent_y(step, i, part)
                sent_c(step, i, part)
    gather_end(0)
    gather_end(1)
    for save in saves:
        save.wait()


TILE = 1024
PART = 256


def angles():
    theta = (np.arange(NTH, dtype=np.float64)[:, None] + 0.5) * (math.pi / 2.0 / NTH)
    phi = (np.arange(NPH // 4, dtype=np.float64)[None, :] + 0.5) * (2.0 * math.pi / NPH)
    ux = (np.sin(theta) * np.cos(phi)).reshape(-1)
    uy = (np.sin(theta) * np.sin(phi)).reshape(-1)
    return ux, uy


def tiled(rows):
    return np.ascontiguousarray(rows.reshape(rows.shape[0], -1, TILE).swapaxes(0, 1))


def make_seeds(nx, ny):
    ux, uy = angles()
    x0, y0 = (nx - 1) / 2.0, (ny - 1) / 2.0
    rows = []
    for length in WAVELENGTHS:
        wave = 2.0 * math.pi / length
        turns = [(y0 - y) * uy for y in range(8)]
        rows += [np.cos(wave * angle) for angle in turns] + [np.sin(wave * angle) for angle in turns]
        for angle in (x0 * ux, (x0 - 1.0) * ux, -2.0 * ux, x0 * ux + y0 * uy, x0 * ux - y0 * uy, -8.0 * uy, -16.0 * uy):
            rows += [np.cos(wave * angle), np.sin(wave * angle)]
        rows += [np.zeros_like(ux)] * 2
    return tiled(np.stack(rows).astype(np.float32))


def far_kernel(
    ngx, ngy, nx, ny, g_ref, seeds, e_in, h_in, p_in, far, e_out, h_out, p_out,
    a_high, a_low, e_pass, h_pass, p_pass, sem,
):
    pid = pl.program_id(0)
    half = 2 * nx
    depth = ny // 2
    per = ny // ngy // 8
    fields = enumerate(zip((e_in, h_in, p_in), (e_pass, h_pass, p_pass), (e_out, h_out, p_out)))
    moves = [
        (pltpu.make_async_copy(src, mid, sem.at[0, i]), pltpu.make_async_copy(mid, dst, sem.at[1, i]))
        for i, (src, mid, dst) in fields
    ]

    @pl.when(pid == 0)
    def _():
        for load, _ in moves:
            load.start()
        quarter = lax.broadcasted_iota(jnp.int32, (32, 128), 1) // 32
        for s in range(2):
            for x in range(ngx // 2):
                for group in range(ngy // 8):
                    kinds = [[], [], [], []]
                    for y in range(4 * group, 4 * group + 4):
                        low_x, high_x = x * ngy, (ngx - 1 - x) * ngy
                        t00, t10 = g_ref[s, low_x + y], g_ref[s, high_x + y]
                        t01, t11 = g_ref[s, low_x + ngy - 1 - y], g_ref[s, high_x + ngy - 1 - y]
                        even0, even1, odd0, odd1 = t10 + t00, t11 + t01, t10 - t00, t11 - t01
                        for kind, tile in zip(kinds, (even0 + even1, odd0 + odd1, even1 - even0, odd1 - odd0)):
                            kind.append(tile)
                    turned = jnp.concatenate(kinds[0] + kinds[1] + kinds[2] + kinds[3], axis=0).T
                    for kind in range(4):
                        block = jnp.zeros((32, 128), F32)
                        for yb in range(4):
                            piece = turned[32 * yb : 32 * yb + 32, :]
                            shift = (32 * (yb - kind)) % 128
                            if shift:
                                piece = pltpu.roll(piece, shift, 1)
                            block = jnp.where(quarter == yb, piece, block)
                        high = block.astype(BF16)
                        rows = pl.ds((2 * s + kind % 2) * half + 32 * x, 32)
                        lanes = pl.ds(128 * group, 128)
                        a_high[kind // 2, rows, lanes] = high
                        a_low[kind // 2, rows, lanes] = (block - high.astype(F32)).astype(BF16)

    @pl.when(pid == 1)
    def _():
        for load, save in moves:
            load.wait()
            save.start()

    scale = 1.0 / math.sqrt(nx * ny)
    sub = lax.broadcasted_iota(jnp.int32, (8, PART), 0)
    top = sub < 4
    lane = lax.broadcasted_iota(jnp.int32, (8, 128), 1)
    first = lane < 64
    mirror = 127 - lane

    def times(a, b):
        return (a[0] * b[0] - a[1] * b[1], a[0] * b[1] + a[1] * b[0])

    for o in range(0, TILE, PART):
        lanes = slice(o, o + PART)
        for f in range(2):
            omega = 2.0 * math.pi / WAVELENGTHS[f]
            kappa = [math.cos(omega * (s + 1) * DT) * scale for s in range(2)]
            sigma = [math.sin(omega * (s + 1) * DT) * scale for s in range(2)]

            def seed(i):
                row = 32 * f + 16 + i
                return jnp.broadcast_to(seeds[0, row : row + 1, lanes], (8, PART))

            v = (seeds[0, 32 * f : 32 * f + 8, lanes], seeds[0, 32 * f + 8 : 32 * f + 16, lanes])
            e16 = (seed(12), seed(13))
            w = times(v, (seed(10), seed(11)))
            waves = []
            for j in range(depth // 16):
                waves += [v, w]
                if 16 * (j + 1) < depth:
                    v, w = times(v, e16), times(w, e16)
            order = [
                (4 * group + y) * per + yb for group in range(depth // 128) for yb in range(per) for y in range(4)
            ]
            sums = []
            for trig in range(2):
                full = jnp.concatenate([waves[j][trig] for j in order], axis=0)
                high = full.astype(BF16)
                low = (full - high.astype(F32)).astype(BF16)
                ah, al = a_high[trig], a_low[trig]
                sums.append(jnp.dot(
                    jnp.concatenate([ah, ah, al], axis=1), jnp.concatenate([high, low, high], axis=0),
                    preferred_element_type=F32))
            w = (jnp.where(top, seed(0), seed(2)), jnp.where(top, seed(1), seed(3)))
            e2 = (seed(4), seed(5))
            acc = [[None] * 4, [None] * 4]
            for g in range(nx // 4):
                for s in range(2):
                    for trig in range(2):
                        for odd in range(2):
                            at = (2 * s + odd) * half + 8 * g
                            term = sums[trig][at : at + 8, :] * w[odd]
                            i = 2 * trig + odd
                            acc[s][i] = term if g == 0 else acc[s][i] + term
                if g + 1 < nx // 4:
                    w = times(w, e2)
            ck, sk, dk, rk = [acc[0][i] * kappa[0] + acc[1][i] * kappa[1] for i in range(4)]
            cg, sg, dg, rg = [acc[0][i] * sigma[0] + acc[1][i] * sigma[1] for i in range(4)]
            re_same, re_diff = ck - rk, ck + rk
            im_same, im_diff = cg - rg, cg + rg
            plus_k, minus_k = sk + dk, sk - dk
            plus_g, minus_g = sg + dg, sg - dg
            quads = (
                (re_same + plus_g, plus_k - im_same),
                (re_diff - minus_g, -minus_k - im_diff),
                (re_same - plus_g, -plus_k - im_same),
                (re_diff + minus_g, minus_k - im_diff),
            )
            same = (seed(6), jnp.where(top, -seed(7), seed(7)))
            diff = (seed(8), jnp.where(top, -seed(9), seed(9)))
            done = []
            for q, (re, im) in enumerate(quads):
                both = jnp.where(top, re, im) + pltpu.roll(jnp.where(top, im, re), 4, 0)
                turn = (same, diff)[q % 2]
                swing = pltpu.roll(both, 4, 0) * turn[1]
                done.append(both * turn[0] + (swing if q in (0, 3) else -swing))
            for pair in range(PART // 128):
                cut = slice(128 * pair, 128 * pair + 128)
                for h in range(2):
                    here, back = done[2 * h][:, cut], jnp.take_along_axis(done[2 * h + 1][:, cut], mirror, axis=1)
                    both = (jnp.where(first, here, back), pltpu.roll(jnp.where(first, back, here), 64, 1))
                    for t in range(2):
                        d = (2 * (o // 128 + pair) + t) * 256 + h * 128
                        far[f, 0, :, d : d + 128] = both[t][0:4]
                        far[f, 1, :, d : d + 128] = both[t][4:8]

    @pl.when(pid == pl.num_programs(0) - 1)
    def _():
        for _, save in moves:
            save.wait()


def shards(
    e_field, h_field, polar, polar_prev, material,
    eps_table, delta_table, omega_table, damping_table, surface_flags,
):
    _, cx, cy, nz = e_field.shape
    ngx, ngy = lax.axis_size("gx"), lax.axis_size("gy")
    nx, ny = ngx * cx, ngy * cy
    width = 4 * nx
    hbm = pl.BlockSpec(memory_space=pl.ANY)
    field = jax.ShapeDtypeStruct(e_field.shape, F32)
    dma = pltpu.SemaphoreType.DMA
    e, h, p, g = pl.pallas_call(
        functools.partial(step_kernel, ngx, ngy, eps_table.shape[0]),
        out_shape=(field, field, field, jax.ShapeDtypeStruct((2, ngx * ngy, 8, 128), F32)),
        in_specs=[hbm] * 10,
        out_specs=(hbm,) * 4,
        scratch_shapes=[
            *[pltpu.VMEM(e_field.shape, F32)] * 4,
            pltpu.VMEM((cx, cy, nz), jnp.int32),
            pltpu.VMEM((2, 2, cy, nz), F32),
            pltpu.VMEM((2, 2, 2, cx, 1, nz), F32),
            pltpu.VMEM((2, 2, 1, nz), F32),
            pltpu.VMEM((2, 2, cy, nz), F32),
            pltpu.VMEM((2, 2, cy, nz), F32),
            pltpu.VMEM((2, 2, cx, 1, nz), F32),
            pltpu.VMEM((2, 2, cx, 1, nz), F32),
            pltpu.VMEM((2, 2, 1, nz), F32),
            pltpu.VMEM((2, 8, 128), F32),
            *[pltpu.SMEM(table.shape, F32) for table in (eps_table, delta_table, omega_table, damping_table)],
            pltpu.SMEM(surface_flags.shape, jnp.int32),
            dma((10,)), dma((5,)), *[dma((2, 2, 4))] * 2, *[dma((2, 2, 2))] * 4,
            dma((2, ngx * ngy)), dma((2, ngx * ngy)), pltpu.SemaphoreType.REGULAR,
        ],
        compiler_params=pltpu.CompilerParams(
            collective_id=0, has_side_effects=True, vmem_limit_bytes=58 * 1024 * 1024),
    )(e_field, h_field, polar, polar_prev, material,
      eps_table, delta_table, omega_table, damping_table, surface_flags)

    steps = (NDIR // 4) // TILE
    seeds = make_seeds(nx, ny)
    far, e, h, p = pl.pallas_call(
        functools.partial(far_kernel, ngx, ngy, nx, ny),
        grid=(steps,),
        out_shape=(jax.ShapeDtypeStruct((2, 2, 4, NDIR), F32), field, field, field),
        in_specs=[
            pl.BlockSpec(g.shape, lambda i: (0, 0, 0, 0)),
            pl.BlockSpec((1, *seeds.shape[1:]), lambda i: (i, 0, 0)),
            hbm, hbm, hbm,
        ],
        out_specs=(pl.BlockSpec((2, 2, 4, 4 * TILE), lambda i: (0, 0, 0, i)), hbm, hbm, hbm),
        scratch_shapes=[
            pltpu.VMEM((2, 2 * width, ny // 2), BF16),
            pltpu.VMEM((2, 2 * width, ny // 2), BF16),
            *[pltpu.VMEM(e_field.shape, F32)] * 3,
            dma((2, 3)),
        ],
        compiler_params=pltpu.CompilerParams(vmem_limit_bytes=56 * 1024 * 1024),
    )(g, jnp.asarray(seeds), e, h, p)
    return e, h, p, far


def solution(mesh):
    cells = P(None, "gx", "gy", None)
    placed = (cells, cells, cells, cells, P("gx", "gy", None), P(), P(), P(), P(), P("gx", "gy"))
    return jax.shard_map(
        shards, mesh=mesh, in_specs=placed, out_specs=(cells, cells, cells, P()), check_vma=False,
    )
```

```python
import functools
import math

import jax
import jax.numpy as jnp
import numpy as np
from jax import lax
from jax.experimental import pallas as pl
from jax.experimental.pallas import tpu as pltpu
from jax.sharding import PartitionSpec as P

NTH = 64
NPH = 256
NDIR = 16384
ZS = 384
DT = 0.55
WAVELENGTHS = (5.0, 4.0)
MESH = pl.DeviceIdType.MESH
F32 = jnp.float32
BF16 = jnp.bfloat16
BY = 8
H_PARTS = (((128, 512), (0, 128)), ((256, 512), (0, 256)))
E_PARTS = (((256, 512), (0, 256)), ((384, 512), (0, 384)))


def coefficients(nmat, nz, eps, delta, omega, damping):
    coef = []
    for m in range(nmat):
        half = jnp.full((1, nz), damping[m], F32) * (DT / 2.0)
        denom = 1.0 + half
        om = jnp.full((1, nz), omega[m], F32)
        square = om * om * (DT * DT)
        coef.append((
            (2.0 - square) / denom,
            (half - 1.0) / denom,
            jnp.full((1, nz), delta[m], F32) * square / denom,
            1.0 / jnp.full((1, nz), eps[m], F32),
        ))
    return coef


def step_kernel(
    ngx, ngy, nmat,
    e_in, h_in, p_in, q_in, m_in, eps_in, delta_in, omega_in, damping_in, flags_in,
    e_out, h_out, p_out, g_out,
    E, H, PA, PB, MAT, xstage, ystage, cstage, xe, xh, ye, yh, ce, G, eps, delta, omega, damping, flags,
    in_sem, out_sem, xs_sem, xr_sem, ys_sem, yr_sem, cs_sem, cr_sem, g1s, g1r, all_in,
):
    cx, cy, nz = MAT.shape
    gx = lax.axis_index("gx")
    gy = lax.axis_index("gy")

    inner, lower = pl.ds(1, cx - 2), pl.ds(0, cx - 1)
    pairs = [
        (e_in.at[:, 0], E.at[:, 0]), (e_in.at[:, cx - 1], E.at[:, cx - 1]), (h_in.at[:, cx - 1], H.at[:, cx - 1]),
        (e_in.at[:, inner], E.at[:, inner]), (h_in.at[:, lower], H.at[:, lower]),
        (p_in, PA), (q_in, PB), (m_in, MAT),
        (eps_in, eps), (delta_in, delta), (omega_in, omega), (damping_in, damping), (flags_in, flags),
    ]
    loads = [pltpu.make_async_copy(src, dst, in_sem.at[i]) for i, (src, dst) in enumerate(pairs)]
    for load in loads[:5] + loads[8:]:
        load.start()

    barrier = pltpu.get_barrier_semaphore()
    for k in range(1, ngx):
        pl.semaphore_signal(barrier, inc=1, device_id=(lax.rem(gx + k, ngx), gy), device_id_type=MESH)
    for k in range(1, ngy):
        pl.semaphore_signal(barrier, inc=1, device_id=(gx, lax.rem(gy + k, ngy)), device_id_type=MESH)

    for dx, dy in ((1, ngy - 1), (ngx - 1, 1)):
        pl.semaphore_signal(
            barrier, inc=1, device_id=(lax.rem(gx + dx, ngx), lax.rem(gy + dy, ngy)), device_id_type=MESH)

    not_low_x, not_high_x = gx > 0, gx < ngx - 1
    not_low_y, not_high_y = gy > 0, gy < ngy - 1
    dt_x = jnp.where(not_low_x, DT, 0.0)
    dt_y = jnp.where(not_low_y, DT, 0.0)

    def clear(ref):
        ref[...] = jnp.zeros(ref.shape, F32)

    pl.when(gx == ngx - 1)(lambda: clear(xe))
    pl.when(gx == 0)(lambda: clear(xh))
    pl.when(gy == ngy - 1)(lambda: clear(ye))
    pl.when(gy == 0)(lambda: clear(yh))
    for kind, there in ((0, not_low_x & not_high_y), (1, not_high_x & not_low_y)):

        @pl.when(jnp.logical_not(there))
        def _():
            for step in range(2):
                ce[step, kind] = jnp.zeros((1, nz), F32)

    sends_x, takes_x = (not_low_x, not_high_x), (not_high_x, not_low_x)
    sends_y, takes_y = (not_low_y, not_high_y), (not_high_y, not_low_y)

    def lanes_of(step, way, part):
        low, high = (H_PARTS, E_PARTS)[way][step][part]
        return pl.ds(low, high - low)

    def x_copies(step, way, part):
        lanes = lanes_of(step, way, part)
        copies = []
        for i in range(2):
            src = E.at[1 + i, 0, :, lanes] if way == 0 else xstage.at[step, i, :, lanes]
            dst = (xe, xh)[way].at[step, i, :, lanes]
            copies.append(pltpu.make_async_remote_copy(
                src_ref=src, dst_ref=dst,
                send_sem=xs_sem.at[step, way, 2 * part + i], recv_sem=xr_sem.at[step, way, 2 * part + i],
                device_id=(lax.rem(gx + (ngx - 1, 1)[way], ngx), gy), device_id_type=MESH))
        return copies

    def y_copy(step, way, part):
        lanes = lanes_of(step, way, part)
        return pltpu.make_async_remote_copy(
            src_ref=ystage.at[step, way, :, :, :, lanes], dst_ref=(ye, yh)[way].at[step, :, :, :, lanes],
            send_sem=ys_sem.at[step, way, part], recv_sem=yr_sem.at[step, way, part],
            device_id=(gx, lax.rem(gy + (ngy - 1, 1)[way], ngy)), device_id_type=MESH)

    sends_c = (not_high_x & not_low_y, not_low_x & not_high_y)
    takes_c = (not_low_x & not_high_y, not_high_x & not_low_y)

    def c_copy(step, kind, part):
        dx, dy = ((1, ngy - 1), (ngx - 1, 1))[kind]
        lanes = lanes_of(step, 1, part)
        return pltpu.make_async_remote_copy(
            src_ref=cstage.at[step, kind, :, lanes], dst_ref=ce.at[step, kind, :, lanes],
            send_sem=cs_sem.at[step, kind, part], recv_sem=cr_sem.at[step, kind, part],
            device_id=(lax.rem(gx + dx, ngx), lax.rem(gy + dy, ngy)), device_id_type=MESH)

    def send_x(step, way, part):
        @pl.when(sends_x[way])
        def _():
            for copy in x_copies(step, way, part):
                copy.start()

    def take_x(step, way, part):
        @pl.when(takes_x[way])
        def _():
            for copy in x_copies(step, way, part):
                copy.wait_recv()

    def sent_x(step, way, part):
        @pl.when(sends_x[way])
        def _():
            for copy in x_copies(step, way, part):
                copy.wait_send()

    def send_y(step, way, part):
        pl.when(sends_y[way])(lambda: y_copy(step, way, part).start())

    def take_y(step, way, part):
        pl.when(takes_y[way])(lambda: y_copy(step, way, part).wait_recv())

    def sent_y(step, way, part):
        pl.when(sends_y[way])(lambda: y_copy(step, way, part).wait_send())

    def send_c(step, part):
        lanes = slice(*E_PARTS[step][part])
        cstage[step, 0, :, lanes] = E[0, cx - 1, 0:1, lanes]
        cstage[step, 1, :, lanes] = E[1, 0, cy - 1 : cy, lanes]
        for kind in range(2):
            pl.when(sends_c[kind])(lambda: c_copy(step, kind, part).start())

    def take_c(step, kind, part):
        pl.when(takes_c[kind])(lambda: c_copy(step, kind, part).wait_recv())

    def sent_c(step, kind, part):
        pl.when(sends_c[kind])(lambda: c_copy(step, kind, part).wait_send())

    blocks = range(cy // BY)
    last = cy // BY - 1

    def ids(span, dim):
        return lax.broadcasted_iota(jnp.int32, (BY, span[1] - span[0]), dim)

    def up_y(v, row, span):
        return jnp.where(ids(span, 0) == BY - 1, row, pltpu.roll(v, BY - 1, 0))

    def down_y(v, row, span):
        return jnp.where(ids(span, 0) == 0, row, pltpu.roll(v, 1, 0))

    def up_z(ref, c, x, here, span):
        low, high = span
        n = high - low
        if high == nz:
            return jnp.where(ids(span, 1) == n - 1, 0.0, pltpu.roll(ref[c, x, here, low:high], n - 1, 1))
        return pltpu.roll(ref[c, x, here, low : high + 128], n + 127, 1)[:, :n]

    def down_z(ref, c, x, here, span):
        low, high = span
        if low == 0:
            return jnp.where(ids(span, 1) == 0, 0.0, pltpu.roll(ref[c, x, here, low:high], 1, 1))
        return pltpu.roll(ref[c, x, here, low - 128 : high], 1, 1)[:, 128:]

    def part_x(step, part):
        span = E_PARTS[step][part]
        lanes, x = slice(*span), cx - 1
        for block in blocks:
            here, y = pl.ds(block * BY, BY), block * BY
            ex, ey, ez = E[0, x, here, lanes], E[1, x, here, lanes], E[2, x, here, lanes]
            rx = E[0, x, y + BY : y + BY + 1, lanes] if block < last else jnp.zeros((1, span[1] - span[0]), F32)
            xstage[step, 0, here, lanes] = H[1, x, here, lanes] - DT * ((up_z(E, 0, x, here, span) - ex) + ez)
            xstage[step, 1, here, lanes] = H[2, x, here, lanes] + DT * (ey + (up_y(ex, rx, span) - ex))
        send_x(step, 1, part)

    def part_y(step, part):
        span = E_PARTS[step][part]
        here, lanes = pl.ds(cy - BY, BY), slice(*span)
        for x in range(cx):
            ex, ey, ez = E[0, x, here, lanes], E[1, x, here, lanes], E[2, x, here, lanes]
            slope = E[1, x + 1, here, lanes] - ey if x < cx - 1 else -ey
            part_hx = H[0, x, here, lanes] + DT * (ez + (up_z(E, 1, x, here, span) - ey))
            part_hz = H[2, x, here, lanes] - DT * (slope + ex)
            ystage[step, 1, 0, x, :, lanes] = part_hx[BY - 1 : BY, :]
            ystage[step, 1, 1, x, :, lanes] = part_hz[BY - 1 : BY, :]
        send_y(step, 1, part)

    def rows_y(step, part):
        lanes = slice(*H_PARTS[step][part])
        for i, c in enumerate((0, 2)):
            for x in range(cx):
                ystage[step, 0, i, x, :, lanes] = E[c, x, 0:1, lanes]
        send_y(step, 0, part)

    def h_plane(step, x, blocks, span):
        lanes = slice(*span)
        for y in [BY * block for block in blocks]:
            here = pl.ds(y, BY)
            ex, ey, ez = E[0, x, here, lanes], E[1, x, here, lanes], E[2, x, here, lanes]
            if y + BY < cy:
                rx, rz = E[0, x, y + BY : y + BY + 1, lanes], E[2, x, y + BY : y + BY + 1, lanes]
            else:
                rx, rz = ye[step, 0, x, :, lanes], ye[step, 1, x, :, lanes]
            if isinstance(x, int) and x == cx - 1:
                eyx, ezx = xe[step, 0, here, lanes], xe[step, 1, here, lanes]
            else:
                eyx, ezx = E[1, x + 1, here, lanes], E[2, x + 1, here, lanes]
            curl_x = (up_y(ez, rz, span) - ez) - (up_z(E, 1, x, here, span) - ey)
            curl_y = (up_z(E, 0, x, here, span) - ex) - (ezx - ez)
            curl_z = (eyx - ey) - (up_y(ex, rx, span) - ex)
            H[0, x, here, lanes] = H[0, x, here, lanes] - DT * curl_x
            H[1, x, here, lanes] = H[1, x, here, lanes] - DT * curl_y
            H[2, x, here, lanes] = H[2, x, here, lanes] - DT * curl_z

    def e_plane(step, x, coef, blocks, span):
        now, old = (PA, PB) if step == 0 else (PB, PA)
        fixed = isinstance(x, int)
        lanes, n = slice(*span), span[1] - span[0]
        for y in [BY * block for block in blocks]:
            here = pl.ds(y, BY)
            mat = MAT[x, here, lanes]
            vox = [jnp.broadcast_to(coef[nmat - 1][i][:, :n], (BY, n)) for i in range(4)]
            for m in range(nmat - 1):
                hit = mat == m
                vox = [jnp.where(hit, coef[m][i][:, :n], vox[i]) for i in range(4)]
            a, b, c, inv = vox
            hx, hy, hz = H[0, x, here, lanes], H[1, x, here, lanes], H[2, x, here, lanes]
            if y > 0:
                rx, rz = H[0, x, y - 1 : y, lanes], H[2, x, y - 1 : y, lanes]
            else:
                rx = yh[step, 0, x, :, lanes] - dt_y * E[2, x, 0:1, lanes]
                edge = E[0, x, 0:1, lanes]
                if fixed and x == cx - 1:
                    edge = edge - ce[step, 1, :, lanes]
                rz = yh[step, 1, x, :, lanes] + dt_y * edge
            if fixed and x == 0:
                hyx = xh[step, 0, here, lanes] + dt_x * E[2, 0, here, lanes]
                edge = E[1, 0, here, lanes]
                if y + BY == cy:
                    edge = jnp.where(ids(span, 0) == BY - 1, edge - ce[step, 0, :, lanes], edge)
                hzx = xh[step, 1, here, lanes] - dt_x * edge
            else:
                hyx, hzx = H[1, x - 1, here, lanes], H[2, x - 1, here, lanes]
            curls = (
                (hz - down_y(hz, rz, span)) - (hy - down_z(H, 1, x, here, span)),
                (hx - down_z(H, 0, x, here, span)) - (hz - hzx),
                (hy - hyx) - (hx - down_y(hx, rx, span)),
            )
            for i in range(3):
                e, p = E[i, x, here, lanes], now[i, x, here, lanes]
                new = a * p + b * old[i, x, here, lanes] + c * e
                E[i, x, here, lanes] = e + (DT * curls[i] - (new - p)) * inv
                old[i, x, here, lanes] = new

    me = gx * ngy + gy
    count = ngx * ngy
    turn_x, turn_y = 2 * gx >= ngx, 2 * gy >= ngy
    tile_lane = lax.broadcasted_iota(jnp.int32, (8, 128), 1)
    tile_row = lax.broadcasted_iota(jnp.int32, (8, 128), 0)

    def surface(step, flag):
        def body(x, acc):
            at = jnp.where(turn_x, cx - 1 - x, x) * 4
            for yb in range(cy // 8):
                base = jnp.where(turn_y, cy // 8 - 1 - yb, yb) * (4 * cx) + at
                rows = slice(8 * yb, 8 * yb + 8)
                cols = (
                    -H[1, x, rows, ZS : ZS + 1], H[0, x, rows, ZS : ZS + 1],
                    E[1, x, rows, ZS : ZS + 1], -E[0, x, rows, ZS : ZS + 1],
                )
                for j in range(4):
                    acc = jnp.where(tile_lane == base + j, cols[j], acc)
            return acc

        tile = lax.fori_loop(0, cx, body, jnp.zeros((8, 128), F32)) * flag
        back = tile
        for bit in (1, 2, 4):
            back = jnp.where((tile_row & bit) != 0, pltpu.roll(back, bit, 0), pltpu.roll(back, 8 - bit, 0))
        G[step] = jnp.where(turn_y, back, tile)

    def peer(step, k):
        to = lax.rem(me + k, count)
        return pltpu.make_async_remote_copy(
            src_ref=G.at[step], dst_ref=g_out.at[step, me], send_sem=g1s.at[step, k], recv_sem=g1r.at[step, k],
            device_id=(to // ngy, lax.rem(to, ngy)), device_id_type=MESH)

    def own(step):
        return pltpu.make_async_copy(G.at[step], g_out.at[step, me], out_sem.at[3 + step])

    def gather_start(step):
        own(step).start()

        for k in range(1, count):
            peer(step, k).start()

    def gather_end(step):
        own(step).wait()

        @pl.loop(1, count)
        def _(k):
            peer(step, k).wait()

    every = (0, nz)
    loads[0].wait()
    pl.semaphore_wait(barrier, ngx + ngy)
    send_x(0, 0, 0)
    loads[1].wait()
    send_c(0, 0)
    loads[2].wait()
    part_x(0, 0)
    send_x(0, 0, 1)
    loads[3].wait()
    rows_y(0, 0)
    loads[4].wait()
    for load in loads[5:8]:
        load.start()
    part_y(0, 0)
    send_c(0, 1)
    part_x(0, 1)
    rows_y(0, 1)
    part_y(0, 1)
    for k in range(1, ngy):
        pl.semaphore_signal(all_in, inc=1, device_id=(gx, lax.rem(gy + k, ngy)), device_id_type=MESH)
    for load in loads[8:]:
        load.wait()

    coef = coefficients(nmat, nz, eps, delta, omega, damping)
    flag = flags[0, 0].astype(F32)

    for step in range(2):

        @pl.loop(0, cx - 1)
        def _(x):
            h_plane(step, x, range(last), every)

        if step == 0:
            for load in loads[5:8]:
                load.wait()
        else:
            gather_start(0)

        @pl.loop(1, cx - 1)
        def _(x):
            e_plane(step, x, coef, range(1, last), every)

        for part in range(2):
            h_span, e_span = H_PARTS[step][part], E_PARTS[step][part]
            take_y(step, 0, part)

            @pl.loop(0, cx - 1)
            def _(x):
                h_plane(step, x, [last], h_span)

            take_x(step, 0, part)
            h_plane(step, cx - 1, blocks, h_span)
            if step == 1 and part == 1:
                pltpu.make_async_copy(H, h_out, out_sem.at[0]).start()
            sent_x(step, 0, part)
            take_y(step, 1, part)
            take_c(step, 1, part)
            e_plane(step, cx - 1, coef, blocks, e_span)
            if step == 0:
                part_x(1, part)
            take_x(step, 1, part)
            take_c(step, 0, part)
            e_plane(step, 0, coef, blocks, e_span)
            if step == 0:
                send_x(1, 0, part)
                send_c(1, part)

            @pl.loop(1, cx - 1)
            def _(x):
                e_plane(step, x, coef, [0, last], e_span)

            if step == 0:
                rows_y(1, part)
                part_y(1, part)
            elif part == 0:
                surface(1, flag)
                gather_start(1)
        if step == 0:
            surface(0, flag)
            pl.semaphore_wait(all_in, ngy - 1)

    saves = [
        pltpu.make_async_copy(H, h_out, out_sem.at[0]),
        pltpu.make_async_copy(E, e_out, out_sem.at[1]),
        pltpu.make_async_copy(PA, p_out, out_sem.at[2]),
    ]
    saves[1].start()
    saves[2].start()
    for step in range(2):
        for part in range(2):
            sent_x(step, 1, part)
            for i in range(2):
                sent_y(step, i, part)
                sent_c(step, i, part)
    gather_end(0)
    gather_end(1)
    for save in saves:
        save.wait()


TILE = 1024
PART = 256


def angles():
    theta = (np.arange(NTH, dtype=np.float64)[:, None] + 0.5) * (math.pi / 2.0 / NTH)
    phi = (np.arange(NPH // 4, dtype=np.float64)[None, :] + 0.5) * (2.0 * math.pi / NPH)
    ux = (np.sin(theta) * np.cos(phi)).reshape(-1)
    uy = (np.sin(theta) * np.sin(phi)).reshape(-1)
    return ux, uy


def tiled(rows):
    return np.ascontiguousarray(rows.reshape(rows.shape[0], -1, TILE).swapaxes(0, 1))


def make_seeds(nx, ny):
    ux, uy = angles()
    x0, y0 = (nx - 1) / 2.0, (ny - 1) / 2.0
    rows = []
    for length in WAVELENGTHS:
        wave = 2.0 * math.pi / length
        turns = [(y0 - y) * uy for y in range(8)]
        rows += [np.cos(wave * angle) for angle in turns] + [np.sin(wave * angle) for angle in turns]
        for angle in (x0 * ux, (x0 - 1.0) * ux, -2.0 * ux, x0 * ux + y0 * uy, x0 * ux - y0 * uy, -8.0 * uy, -16.0 * uy):
            rows += [np.cos(wave * angle), np.sin(wave * angle)]
        rows += [np.zeros_like(ux)] * 2
    return tiled(np.stack(rows).astype(np.float32))


def far_kernel(
    ngx, ngy, nx, ny, g_in, seeds_in, e_in, h_in, p_in, far_out, e_out, h_out, p_out,
    g_ref, seeds, far, a_high, a_low, e_pass, h_pass, p_pass, sem, seed_sem, far_sem, g_sem,
):
    half = 2 * nx
    depth = ny // 2
    per = ny // ngy // 8
    tiles = seeds.shape[0]
    g_load = pltpu.make_async_copy(g_in, g_ref, g_sem)
    g_load.start()

    def seed_load(tile):
        return pltpu.make_async_copy(seeds_in.at[tile], seeds.at[tile], seed_sem.at[tile])

    def far_save(tile):
        lanes = pl.ds(pl.multiple_of(tile * 4 * TILE, 4 * TILE), 4 * TILE)
        return pltpu.make_async_copy(far.at[tile], far_out.at[:, :, :, lanes], far_sem.at[tile])

    for tile in range(tiles):
        seed_load(tile).start()
    fields = enumerate(zip((e_in, h_in, p_in), (e_pass, h_pass, p_pass), (e_out, h_out, p_out)))
    moves = [
        (pltpu.make_async_copy(src, mid, sem.at[0, i]), pltpu.make_async_copy(mid, dst, sem.at[1, i]))
        for i, (src, mid, dst) in fields
    ]
    g_load.wait()
    quarter = lax.broadcasted_iota(jnp.int32, (32, 128), 1) // 32
    for s in range(2):
        for x in range(ngx // 2):
            for group in range(ngy // 8):
                kinds = [[], [], [], []]
                for y in range(4 * group, 4 * group + 4):
                    low_x, high_x = x * ngy, (ngx - 1 - x) * ngy
                    t00, t10 = g_ref[s, low_x + y], g_ref[s, high_x + y]
                    t01, t11 = g_ref[s, low_x + ngy - 1 - y], g_ref[s, high_x + ngy - 1 - y]
                    even0, even1, odd0, odd1 = t10 + t00, t11 + t01, t10 - t00, t11 - t01
                    for kind, tile in zip(kinds, (even0 + even1, odd0 + odd1, even1 - even0, odd1 - odd0)):
                        kind.append(tile)
                turned = jnp.concatenate(kinds[0] + kinds[1] + kinds[2] + kinds[3], axis=0).T
                for kind in range(4):
                    block = jnp.zeros((32, 128), F32)
                    for yb in range(4):
                        piece = turned[32 * yb : 32 * yb + 32, :]
                        shift = (32 * (yb - kind)) % 128
                        if shift:
                            piece = pltpu.roll(piece, shift, 1)
                        block = jnp.where(quarter == yb, piece, block)
                    high = block.astype(BF16)
                    rows = pl.ds((2 * s + kind % 2) * half + 32 * x, 32)
                    lanes = pl.ds(128 * group, 128)
                    a_high[kind // 2, rows, lanes] = high
                    a_low[kind // 2, rows, lanes] = (block - high.astype(F32)).astype(BF16)

    scale = 1.0 / math.sqrt(nx * ny)
    sub = lax.broadcasted_iota(jnp.int32, (8, PART), 0)
    top = sub < 4
    lane = lax.broadcasted_iota(jnp.int32, (8, 128), 1)
    first = lane < 64
    mirror = 127 - lane

    def times(a, b):
        return (a[0] * b[0] - a[1] * b[1], a[0] * b[1] + a[1] * b[0])

    @pl.loop(0, tiles)
    def _(tile):
        seed_load(tile).wait()

        @pl.when(tile == 0)
        def _():
            for load, _ in moves:
                load.start()

        @pl.when(tile == 2)
        def _():
            for load, save in moves:
                load.wait()
                save.start()

        for o in range(0, TILE, PART):
            lanes = slice(o, o + PART)
            for f in range(2):
                omega = 2.0 * math.pi / WAVELENGTHS[f]
                kappa = [math.cos(omega * (s + 1) * DT) * scale for s in range(2)]
                sigma = [math.sin(omega * (s + 1) * DT) * scale for s in range(2)]

                def seed(i):
                    row = 32 * f + 16 + i
                    return jnp.broadcast_to(seeds[tile, row : row + 1, lanes], (8, PART))

                v = (seeds[tile, 32 * f : 32 * f + 8, lanes], seeds[tile, 32 * f + 8 : 32 * f + 16, lanes])
                e16 = (seed(12), seed(13))
                w = times(v, (seed(10), seed(11)))
                waves = []
                for j in range(depth // 16):
                    waves += [v, w]
                    if 16 * (j + 1) < depth:
                        v, w = times(v, e16), times(w, e16)
                order = [
                    (4 * group + y) * per + yb for group in range(depth // 128) for yb in range(per) for y in range(4)
                ]
                sums = []
                for trig in range(2):
                    full = jnp.concatenate([waves[j][trig] for j in order], axis=0)
                    high = full.astype(BF16)
                    low = (full - high.astype(F32)).astype(BF16)
                    ah, al = a_high[trig], a_low[trig]
                    sums.append(jnp.dot(
                        jnp.concatenate([ah, ah, al], axis=1), jnp.concatenate([high, low, high], axis=0),
                        preferred_element_type=F32))
                w = (jnp.where(top, seed(0), seed(2)), jnp.where(top, seed(1), seed(3)))
                e2 = (seed(4), seed(5))
                acc = [[None] * 4, [None] * 4]
                for g in range(nx // 4):
                    for s in range(2):
                        for trig in range(2):
                            for odd in range(2):
                                at = (2 * s + odd) * half + 8 * g
                                term = sums[trig][at : at + 8, :] * w[odd]
                                i = 2 * trig + odd
                                acc[s][i] = term if g == 0 else acc[s][i] + term
                    if g + 1 < nx // 4:
                        w = times(w, e2)
                ck, sk, dk, rk = [acc[0][i] * kappa[0] + acc[1][i] * kappa[1] for i in range(4)]
                cg, sg, dg, rg = [acc[0][i] * sigma[0] + acc[1][i] * sigma[1] for i in range(4)]
                re_same, re_diff = ck - rk, ck + rk
                im_same, im_diff = cg - rg, cg + rg
                plus_k, minus_k = sk + dk, sk - dk
                plus_g, minus_g = sg + dg, sg - dg
                quads = (
                    (re_same + plus_g, plus_k - im_same),
                    (re_diff - minus_g, -minus_k - im_diff),
                    (re_same - plus_g, -plus_k - im_same),
                    (re_diff + minus_g, minus_k - im_diff),
                )
                same = (seed(6), jnp.where(top, -seed(7), seed(7)))
                diff = (seed(8), jnp.where(top, -seed(9), seed(9)))
                done = []
                for q, (re, im) in enumerate(quads):
                    both = jnp.where(top, re, im) + pltpu.roll(jnp.where(top, im, re), 4, 0)
                    turn = (same, diff)[q % 2]
                    swing = pltpu.roll(both, 4, 0) * turn[1]
                    done.append(both * turn[0] + (swing if q in (0, 3) else -swing))
                for pair in range(PART // 128):
                    cut = slice(128 * pair, 128 * pair + 128)
                    for h in range(2):
                        here, back = done[2 * h][:, cut], jnp.take_along_axis(done[2 * h + 1][:, cut], mirror, axis=1)
                        both = (jnp.where(first, here, back), pltpu.roll(jnp.where(first, back, here), 64, 1))
                        for t in range(2):
                            d = (2 * (o // 128 + pair) + t) * 256 + h * 128
                            far[tile, f, 0, :, d : d + 128] = both[t][0:4]
                            far[tile, f, 1, :, d : d + 128] = both[t][4:8]
        far_save(tile).start()

    @pl.loop(0, tiles)
    def _(tile):
        far_save(tile).wait()

    for _, save in moves:
        save.wait()


def shards(
    e_field, h_field, polar, polar_prev, material,
    eps_table, delta_table, omega_table, damping_table, surface_flags,
):
    _, cx, cy, nz = e_field.shape
    ngx, ngy = lax.axis_size("gx"), lax.axis_size("gy")
    nx, ny = ngx * cx, ngy * cy
    width = 4 * nx
    hbm = pl.BlockSpec(memory_space=pl.ANY)
    field = jax.ShapeDtypeStruct(e_field.shape, F32)
    dma = pltpu.SemaphoreType.DMA
    e, h, p, g = pl.pallas_call(
        functools.partial(step_kernel, ngx, ngy, eps_table.shape[0]),
        out_shape=(field, field, field, jax.ShapeDtypeStruct((2, ngx * ngy, 8, 128), F32)),
        in_specs=[hbm] * 10,
        out_specs=(hbm,) * 4,
        scratch_shapes=[
            *[pltpu.VMEM(e_field.shape, F32)] * 4,
            pltpu.VMEM((cx, cy, nz), jnp.int32),
            pltpu.VMEM((2, 2, cy, nz), F32),
            pltpu.VMEM((2, 2, 2, cx, 1, nz), F32),
            pltpu.VMEM((2, 2, 1, nz), F32),
            pltpu.VMEM((2, 2, cy, nz), F32),
            pltpu.VMEM((2, 2, cy, nz), F32),
            pltpu.VMEM((2, 2, cx, 1, nz), F32),
            pltpu.VMEM((2, 2, cx, 1, nz), F32),
            pltpu.VMEM((2, 2, 1, nz), F32),
            pltpu.VMEM((2, 8, 128), F32),
            *[pltpu.SMEM(table.shape, F32) for table in (eps_table, delta_table, omega_table, damping_table)],
            pltpu.SMEM(surface_flags.shape, jnp.int32),
            dma((13,)), dma((5,)), *[dma((2, 2, 4))] * 2, *[dma((2, 2, 2))] * 4,
            dma((2, ngx * ngy)), dma((2, ngx * ngy)), pltpu.SemaphoreType.REGULAR,
        ],
        compiler_params=pltpu.CompilerParams(
            collective_id=0, has_side_effects=True, vmem_limit_bytes=58 * 1024 * 1024),
    )(e_field, h_field, polar, polar_prev, material,
      eps_table, delta_table, omega_table, damping_table, surface_flags)

    steps = (NDIR // 4) // TILE
    seeds = make_seeds(nx, ny)
    far, e, h, p = pl.pallas_call(
        functools.partial(far_kernel, ngx, ngy, nx, ny),
        out_shape=(jax.ShapeDtypeStruct((2, 2, 4, NDIR), F32), field, field, field),
        in_specs=[hbm] * 5,
        out_specs=(hbm,) * 4,
        scratch_shapes=[
            pltpu.VMEM(g.shape, F32),
            pltpu.VMEM(seeds.shape, F32),
            pltpu.VMEM((steps, 2, 2, 4, 4 * TILE), F32),
            pltpu.VMEM((2, 2 * width, ny // 2), BF16),
            pltpu.VMEM((2, 2 * width, ny // 2), BF16),
            *[pltpu.VMEM(e_field.shape, F32)] * 3,
            dma((2, 3)), dma((steps,)), dma((steps,)), dma,
        ],
        compiler_params=pltpu.CompilerParams(vmem_limit_bytes=56 * 1024 * 1024),
    )(g, jnp.asarray(seeds), e, h, p)
    return e, h, p, far


def solution(mesh):
    cells = P(None, "gx", "gy", None)
    placed = (cells, cells, cells, cells, P("gx", "gy", None), P(), P(), P(), P(), P("gx", "gy"))
    return jax.shard_map(
        shards, mesh=mesh, in_specs=placed, out_specs=(cells, cells, cells, P()), check_vma=False,
    )
```

```python
import functools
import math

import jax
import jax.numpy as jnp
import numpy as np
from jax import lax
from jax.experimental import pallas as pl
from jax.experimental.pallas import tpu as pltpu
from jax.sharding import PartitionSpec as P

NTH = 64
NPH = 256
NDIR = 16384
ZS = 384
DT = 0.55
WAVELENGTHS = (5.0, 4.0)
MESH = pl.DeviceIdType.MESH
F32 = jnp.float32
BF16 = jnp.bfloat16
BY = 8
H_PARTS = (((128, 512), (0, 128)), ((256, 512), (0, 256)))
E_PARTS = (((256, 512), (0, 256)), ((384, 512), (0, 384)))


def coefficients(nmat, nz, eps, delta, omega, damping):
    coef = []
    for m in range(nmat):
        half = jnp.full((1, nz), damping[m], F32) * (DT / 2.0)
        denom = 1.0 + half
        om = jnp.full((1, nz), omega[m], F32)
        square = om * om * (DT * DT)
        coef.append((
            (2.0 - square) / denom,
            (half - 1.0) / denom,
            jnp.full((1, nz), delta[m], F32) * square / denom,
            1.0 / jnp.full((1, nz), eps[m], F32),
        ))
    return coef


def step_kernel(
    ngx, ngy, nmat,
    e_in, h_in, p_in, q_in, m_in, eps_in, delta_in, omega_in, damping_in, flags_in,
    e_out, h_out, p_out, g_out,
    E, H, PA, PB, MAT, xstage, ystage, cstage, xe, xh, ye, yh, ce, G, eps, delta, omega, damping, flags,
    in_sem, out_sem, xs_sem, xr_sem, ys_sem, yr_sem, cs_sem, cr_sem, g1s, g1r, all_in,
):
    cx, cy, nz = MAT.shape
    gx = lax.axis_index("gx")
    gy = lax.axis_index("gy")

    inner, lower = pl.ds(1, cx - 2), pl.ds(0, cx - 1)
    pairs = [
        (e_in.at[:, 0], E.at[:, 0]), (e_in.at[:, cx - 1], E.at[:, cx - 1]), (h_in.at[:, cx - 1], H.at[:, cx - 1]),
        (e_in.at[:, inner], E.at[:, inner]), (h_in.at[:, lower], H.at[:, lower]),
        (p_in, PA), (q_in, PB), (m_in, MAT),
        (eps_in, eps), (delta_in, delta), (omega_in, omega), (damping_in, damping), (flags_in, flags),
    ]
    loads = [pltpu.make_async_copy(src, dst, in_sem.at[i]) for i, (src, dst) in enumerate(pairs)]
    for load in loads[:5] + loads[8:]:
        load.start()

    barrier = pltpu.get_barrier_semaphore()
    for k in range(1, ngx):
        pl.semaphore_signal(barrier, inc=1, device_id=(lax.rem(gx + k, ngx), gy), device_id_type=MESH)
    for k in range(1, ngy):
        pl.semaphore_signal(barrier, inc=1, device_id=(gx, lax.rem(gy + k, ngy)), device_id_type=MESH)

    for dx, dy in ((1, ngy - 1), (ngx - 1, 1)):
        pl.semaphore_signal(
            barrier, inc=1, device_id=(lax.rem(gx + dx, ngx), lax.rem(gy + dy, ngy)), device_id_type=MESH)

    not_low_x, not_high_x = gx > 0, gx < ngx - 1
    not_low_y, not_high_y = gy > 0, gy < ngy - 1
    dt_x = jnp.where(not_low_x, DT, 0.0)
    dt_y = jnp.where(not_low_y, DT, 0.0)

    def clear(ref):
        ref[...] = jnp.zeros(ref.shape, F32)

    pl.when(gx == ngx - 1)(lambda: clear(xe))
    pl.when(gx == 0)(lambda: clear(xh))
    pl.when(gy == ngy - 1)(lambda: clear(ye))
    pl.when(gy == 0)(lambda: clear(yh))
    for kind, there in ((0, not_low_x & not_high_y), (1, not_high_x & not_low_y)):

        @pl.when(jnp.logical_not(there))
        def _():
            for step in range(2):
                ce[step, kind] = jnp.zeros((1, nz), F32)

    sends_x, takes_x = (not_low_x, not_high_x), (not_high_x, not_low_x)
    sends_y, takes_y = (not_low_y, not_high_y), (not_high_y, not_low_y)

    def lanes_of(step, way, part):
        low, high = (H_PARTS, E_PARTS)[way][step][part]
        return pl.ds(low, high - low)

    def x_copies(step, way, part):
        lanes = lanes_of(step, way, part)
        copies = []
        for i in range(2):
            src = E.at[1 + i, 0, :, lanes] if way == 0 else xstage.at[step, i, :, lanes]
            dst = (xe, xh)[way].at[step, i, :, lanes]
            copies.append(pltpu.make_async_remote_copy(
                src_ref=src, dst_ref=dst,
                send_sem=xs_sem.at[step, way, 2 * part + i], recv_sem=xr_sem.at[step, way, 2 * part + i],
                device_id=(lax.rem(gx + (ngx - 1, 1)[way], ngx), gy), device_id_type=MESH))
        return copies

    def y_copy(step, way, part):
        lanes = lanes_of(step, way, part)
        return pltpu.make_async_remote_copy(
            src_ref=ystage.at[step, way, :, :, :, lanes], dst_ref=(ye, yh)[way].at[step, :, :, :, lanes],
            send_sem=ys_sem.at[step, way, part], recv_sem=yr_sem.at[step, way, part],
            device_id=(gx, lax.rem(gy + (ngy - 1, 1)[way], ngy)), device_id_type=MESH)

    sends_c = (not_high_x & not_low_y, not_low_x & not_high_y)
    takes_c = (not_low_x & not_high_y, not_high_x & not_low_y)

    def c_copy(step, kind, part):
        dx, dy = ((1, ngy - 1), (ngx - 1, 1))[kind]
        lanes = lanes_of(step, 1, part)
        return pltpu.make_async_remote_copy(
            src_ref=cstage.at[step, kind, :, lanes], dst_ref=ce.at[step, kind, :, lanes],
            send_sem=cs_sem.at[step, kind, part], recv_sem=cr_sem.at[step, kind, part],
            device_id=(lax.rem(gx + dx, ngx), lax.rem(gy + dy, ngy)), device_id_type=MESH)

    def send_x(step, way, part):
        @pl.when(sends_x[way])
        def _():
            for copy in x_copies(step, way, part):
                copy.start()

    def take_x(step, way, part):
        @pl.when(takes_x[way])
        def _():
            for copy in x_copies(step, way, part):
                copy.wait_recv()

    def sent_x(step, way, part):
        @pl.when(sends_x[way])
        def _():
            for copy in x_copies(step, way, part):
                copy.wait_send()

    def send_y(step, way, part):
        pl.when(sends_y[way])(lambda: y_copy(step, way, part).start())

    def take_y(step, way, part):
        pl.when(takes_y[way])(lambda: y_copy(step, way, part).wait_recv())

    def sent_y(step, way, part):
        pl.when(sends_y[way])(lambda: y_copy(step, way, part).wait_send())

    def send_c(step, part):
        lanes = slice(*E_PARTS[step][part])
        cstage[step, 0, :, lanes] = E[0, cx - 1, 0:1, lanes]
        cstage[step, 1, :, lanes] = E[1, 0, cy - 1 : cy, lanes]
        for kind in range(2):
            pl.when(sends_c[kind])(lambda: c_copy(step, kind, part).start())

    def take_c(step, kind, part):
        pl.when(takes_c[kind])(lambda: c_copy(step, kind, part).wait_recv())

    def sent_c(step, kind, part):
        pl.when(sends_c[kind])(lambda: c_copy(step, kind, part).wait_send())

    blocks = range(cy // BY)
    last = cy // BY - 1

    def ids(span, dim):
        return lax.broadcasted_iota(jnp.int32, (BY, span[1] - span[0]), dim)

    def up_y(v, row, span):
        return jnp.where(ids(span, 0) == BY - 1, row, pltpu.roll(v, BY - 1, 0))

    def down_y(v, row, span):
        return jnp.where(ids(span, 0) == 0, row, pltpu.roll(v, 1, 0))

    def up_z(ref, c, x, here, span):
        low, high = span
        n = high - low
        if high == nz:
            return jnp.where(ids(span, 1) == n - 1, 0.0, pltpu.roll(ref[c, x, here, low:high], n - 1, 1))
        return pltpu.roll(ref[c, x, here, low : high + 128], n + 127, 1)[:, :n]

    def down_z(ref, c, x, here, span):
        low, high = span
        if low == 0:
            return jnp.where(ids(span, 1) == 0, 0.0, pltpu.roll(ref[c, x, here, low:high], 1, 1))
        return pltpu.roll(ref[c, x, here, low - 128 : high], 1, 1)[:, 128:]

    def part_x(step, part):
        span = E_PARTS[step][part]
        lanes, x = slice(*span), cx - 1
        for block in blocks:
            here, y = pl.ds(block * BY, BY), block * BY
            ex, ey, ez = E[0, x, here, lanes], E[1, x, here, lanes], E[2, x, here, lanes]
            rx = E[0, x, y + BY : y + BY + 1, lanes] if block < last else jnp.zeros((1, span[1] - span[0]), F32)
            xstage[step, 0, here, lanes] = H[1, x, here, lanes] - DT * ((up_z(E, 0, x, here, span) - ex) + ez)
            xstage[step, 1, here, lanes] = H[2, x, here, lanes] + DT * (ey + (up_y(ex, rx, span) - ex))
        send_x(step, 1, part)

    def part_y(step, part):
        span = E_PARTS[step][part]
        here, lanes = pl.ds(cy - BY, BY), slice(*span)
        for x in range(cx):
            ex, ey, ez = E[0, x, here, lanes], E[1, x, here, lanes], E[2, x, here, lanes]
            slope = E[1, x + 1, here, lanes] - ey if x < cx - 1 else -ey
            part_hx = H[0, x, here, lanes] + DT * (ez + (up_z(E, 1, x, here, span) - ey))
            part_hz = H[2, x, here, lanes] - DT * (slope + ex)
            ystage[step, 1, 0, x, :, lanes] = part_hx[BY - 1 : BY, :]
            ystage[step, 1, 1, x, :, lanes] = part_hz[BY - 1 : BY, :]
        send_y(step, 1, part)

    def rows_y(step, part):
        lanes = slice(*H_PARTS[step][part])
        for i, c in enumerate((0, 2)):
            for x in range(cx):
                ystage[step, 0, i, x, :, lanes] = E[c, x, 0:1, lanes]
        send_y(step, 0, part)

    def h_plane(step, x, blocks, span):
        lanes = slice(*span)
        for y in [BY * block for block in blocks]:
            here = pl.ds(y, BY)
            ex, ey, ez = E[0, x, here, lanes], E[1, x, here, lanes], E[2, x, here, lanes]
            if y + BY < cy:
                rx, rz = E[0, x, y + BY : y + BY + 1, lanes], E[2, x, y + BY : y + BY + 1, lanes]
            else:
                rx, rz = ye[step, 0, x, :, lanes], ye[step, 1, x, :, lanes]
            if isinstance(x, int) and x == cx - 1:
                eyx, ezx = xe[step, 0, here, lanes], xe[step, 1, here, lanes]
            else:
                eyx, ezx = E[1, x + 1, here, lanes], E[2, x + 1, here, lanes]
            curl_x = (up_y(ez, rz, span) - ez) - (up_z(E, 1, x, here, span) - ey)
            curl_y = (up_z(E, 0, x, here, span) - ex) - (ezx - ez)
            curl_z = (eyx - ey) - (up_y(ex, rx, span) - ex)
            H[0, x, here, lanes] = H[0, x, here, lanes] - DT * curl_x
            H[1, x, here, lanes] = H[1, x, here, lanes] - DT * curl_y
            H[2, x, here, lanes] = H[2, x, here, lanes] - DT * curl_z

    def e_plane(step, x, coef, blocks, span):
        now, old = (PA, PB) if step == 0 else (PB, PA)
        fixed = isinstance(x, int)
        lanes, n = slice(*span), span[1] - span[0]
        for y in [BY * block for block in blocks]:
            here = pl.ds(y, BY)
            mat = MAT[x, here, lanes]
            vox = [jnp.broadcast_to(coef[nmat - 1][i][:, :n], (BY, n)) for i in range(4)]
            for m in range(nmat - 1):
                hit = mat == m
                vox = [jnp.where(hit, coef[m][i][:, :n], vox[i]) for i in range(4)]
            a, b, c, inv = vox
            hx, hy, hz = H[0, x, here, lanes], H[1, x, here, lanes], H[2, x, here, lanes]
            if y > 0:
                rx, rz = H[0, x, y - 1 : y, lanes], H[2, x, y - 1 : y, lanes]
            else:
                rx = yh[step, 0, x, :, lanes] - dt_y * E[2, x, 0:1, lanes]
                edge = E[0, x, 0:1, lanes]
                if fixed and x == cx - 1:
                    edge = edge - ce[step, 1, :, lanes]
                rz = yh[step, 1, x, :, lanes] + dt_y * edge
            if fixed and x == 0:
                hyx = xh[step, 0, here, lanes] + dt_x * E[2, 0, here, lanes]
                edge = E[1, 0, here, lanes]
                if y + BY == cy:
                    edge = jnp.where(ids(span, 0) == BY - 1, edge - ce[step, 0, :, lanes], edge)
                hzx = xh[step, 1, here, lanes] - dt_x * edge
            else:
                hyx, hzx = H[1, x - 1, here, lanes], H[2, x - 1, here, lanes]
            curls = (
                (hz - down_y(hz, rz, span)) - (hy - down_z(H, 1, x, here, span)),
                (hx - down_z(H, 0, x, here, span)) - (hz - hzx),
                (hy - hyx) - (hx - down_y(hx, rx, span)),
            )
            for i in range(3):
                e, p = E[i, x, here, lanes], now[i, x, here, lanes]
                new = a * p + b * old[i, x, here, lanes] + c * e
                E[i, x, here, lanes] = e + (DT * curls[i] - (new - p)) * inv
                old[i, x, here, lanes] = new

    me = gx * ngy + gy
    count = ngx * ngy
    turn_x, turn_y = 2 * gx >= ngx, 2 * gy >= ngy
    tile_lane = lax.broadcasted_iota(jnp.int32, (8, 128), 1)
    tile_row = lax.broadcasted_iota(jnp.int32, (8, 128), 0)

    def surface(step, flag):
        def body(x, acc):
            at = jnp.where(turn_x, cx - 1 - x, x) * 4
            for yb in range(cy // 8):
                base = jnp.where(turn_y, cy // 8 - 1 - yb, yb) * (4 * cx) + at
                rows = slice(8 * yb, 8 * yb + 8)
                cols = (
                    -H[1, x, rows, ZS : ZS + 1], H[0, x, rows, ZS : ZS + 1],
                    E[1, x, rows, ZS : ZS + 1], -E[0, x, rows, ZS : ZS + 1],
                )
                for j in range(4):
                    acc = jnp.where(tile_lane == base + j, cols[j], acc)
            return acc

        tile = lax.fori_loop(0, cx, body, jnp.zeros((8, 128), F32)) * flag
        back = tile
        for bit in (1, 2, 4):
            back = jnp.where((tile_row & bit) != 0, pltpu.roll(back, bit, 0), pltpu.roll(back, 8 - bit, 0))
        G[step] = jnp.where(turn_y, back, tile)

    def peer(step, k):
        to = lax.rem(me + k, count)
        return pltpu.make_async_remote_copy(
            src_ref=G.at[step], dst_ref=g_out.at[step, me], send_sem=g1s.at[step, k], recv_sem=g1r.at[step, k],
            device_id=(to // ngy, lax.rem(to, ngy)), device_id_type=MESH)

    def own(step):
        return pltpu.make_async_copy(G.at[step], g_out.at[step, me], out_sem.at[3 + step])

    def gather_start(step):
        own(step).start()

        for k in range(1, count):
            peer(step, k).start()

    def gather_end(step):
        own(step).wait()

        @pl.loop(1, count)
        def _(k):
            peer(step, k).wait()

    every = (0, nz)
    loads[0].wait()
    pl.semaphore_wait(barrier, ngx + ngy)
    send_x(0, 0, 0)
    loads[1].wait()
    send_c(0, 0)
    loads[2].wait()
    part_x(0, 0)
    send_x(0, 0, 1)
    loads[3].wait()
    rows_y(0, 0)
    loads[4].wait()
    for load in loads[5:8]:
        load.start()
    part_y(0, 0)
    send_c(0, 1)
    part_x(0, 1)
    rows_y(0, 1)
    part_y(0, 1)
    for k in range(1, ngy):
        pl.semaphore_signal(all_in, inc=1, device_id=(gx, lax.rem(gy + k, ngy)), device_id_type=MESH)
    for load in loads[8:]:
        load.wait()

    coef = coefficients(nmat, nz, eps, delta, omega, damping)
    flag = flags[0, 0].astype(F32)

    for step in range(2):

        @pl.loop(0, cx - 1)
        def _(x):
            h_plane(step, x, range(last), every)

        if step == 0:
            for load in loads[5:8]:
                load.wait()
        else:
            gather_start(0)

        @pl.loop(1, cx - 1)
        def _(x):
            e_plane(step, x, coef, range(1, last), every)

        for part in range(2):
            h_span, e_span = H_PARTS[step][part], E_PARTS[step][part]
            take_y(step, 0, part)

            @pl.loop(0, cx - 1)
            def _(x):
                h_plane(step, x, [last], h_span)

            take_x(step, 0, part)
            h_plane(step, cx - 1, blocks, h_span)
            if step == 1 and part == 1:
                pltpu.make_async_copy(H, h_out, out_sem.at[0]).start()
            sent_x(step, 0, part)
            take_y(step, 1, part)
            take_c(step, 1, part)
            e_plane(step, cx - 1, coef, blocks, e_span)
            if step == 0:
                part_x(1, part)
            take_x(step, 1, part)
            take_c(step, 0, part)
            e_plane(step, 0, coef, blocks, e_span)
            if step == 0:
                send_x(1, 0, part)
                send_c(1, part)

            @pl.loop(1, cx - 1)
            def _(x):
                e_plane(step, x, coef, [0, last], e_span)

            if step == 0:
                rows_y(1, part)
                part_y(1, part)
            elif part == 0:
                surface(1, flag)
                gather_start(1)
        if step == 0:
            surface(0, flag)
            pl.semaphore_wait(all_in, ngy - 1)

    saves = [
        pltpu.make_async_copy(H, h_out, out_sem.at[0]),
        pltpu.make_async_copy(E, e_out, out_sem.at[1]),
        pltpu.make_async_copy(PA, p_out, out_sem.at[2]),
    ]
    saves[1].start()
    saves[2].start()
    for step in range(2):
        for part in range(2):
            sent_x(step, 1, part)
            for i in range(2):
                sent_y(step, i, part)
                sent_c(step, i, part)
    gather_end(0)
    gather_end(1)
    for save in saves:
        save.wait()


TILE = 2048
PART = 256


def angles():
    theta = (np.arange(NTH, dtype=np.float64)[:, None] + 0.5) * (math.pi / 2.0 / NTH)
    phi = (np.arange(NPH // 4, dtype=np.float64)[None, :] + 0.5) * (2.0 * math.pi / NPH)
    ux = (np.sin(theta) * np.cos(phi)).reshape(-1)
    uy = (np.sin(theta) * np.sin(phi)).reshape(-1)
    return ux, uy


def tiled(rows):
    return np.ascontiguousarray(rows.reshape(rows.shape[0], -1, TILE).swapaxes(0, 1))


def make_seeds(nx, ny):
    ux, uy = angles()
    x0, y0 = (nx - 1) / 2.0, (ny - 1) / 2.0
    rows = []
    for length in WAVELENGTHS:
        wave = 2.0 * math.pi / length
        turns = [(y0 - y) * uy for y in range(8)]
        rows += [np.cos(wave * angle) for angle in turns] + [np.sin(wave * angle) for angle in turns]
        for angle in (x0 * ux, (x0 - 1.0) * ux, -2.0 * ux, x0 * ux + y0 * uy, x0 * ux - y0 * uy, -8.0 * uy, -16.0 * uy):
            rows += [np.cos(wave * angle), np.sin(wave * angle)]
        rows += [np.zeros_like(ux)] * 2
    return tiled(np.stack(rows).astype(np.float32))


def far_kernel(
    ngx, ngy, nx, ny, g_in, seeds_in, e_in, h_in, p_in, far_out, e_out, h_out, p_out,
    g_ref, seeds, far, a_high, a_low, e_pass, h_pass, p_pass, sem, seed_sem, far_sem, g_sem,
):
    half = 2 * nx
    depth = ny // 2
    per = ny // ngy // 8
    tiles = seeds.shape[0]
    g_load = pltpu.make_async_copy(g_in, g_ref, g_sem)
    g_load.start()

    def seed_load(tile):
        return pltpu.make_async_copy(seeds_in.at[tile], seeds.at[tile], seed_sem.at[tile])

    def far_save(tile, i):
        lanes = pl.ds(pl.multiple_of(tile * 4 * TILE + i * 2 * TILE, 2 * TILE), 2 * TILE)
        src = far.at[tile, :, :, :, pl.ds(i * 2 * TILE, 2 * TILE)]
        return pltpu.make_async_copy(src, far_out.at[:, :, :, lanes], far_sem.at[tile, i])

    for tile in range(tiles):
        seed_load(tile).start()
    fields = enumerate(zip((e_in, h_in, p_in), (e_pass, h_pass, p_pass), (e_out, h_out, p_out)))
    moves = [
        (pltpu.make_async_copy(src, mid, sem.at[0, i]), pltpu.make_async_copy(mid, dst, sem.at[1, i]))
        for i, (src, mid, dst) in fields
    ]
    g_load.wait()
    quarter = lax.broadcasted_iota(jnp.int32, (32, 128), 1) // 32
    for s in range(2):
        for x in range(ngx // 2):
            for group in range(ngy // 8):
                kinds = [[], [], [], []]
                for y in range(4 * group, 4 * group + 4):
                    low_x, high_x = x * ngy, (ngx - 1 - x) * ngy
                    t00, t10 = g_ref[s, low_x + y], g_ref[s, high_x + y]
                    t01, t11 = g_ref[s, low_x + ngy - 1 - y], g_ref[s, high_x + ngy - 1 - y]
                    even0, even1, odd0, odd1 = t10 + t00, t11 + t01, t10 - t00, t11 - t01
                    for kind, tile in zip(kinds, (even0 + even1, odd0 + odd1, even1 - even0, odd1 - odd0)):
                        kind.append(tile)
                turned = jnp.concatenate(kinds[0] + kinds[1] + kinds[2] + kinds[3], axis=0).T
                for kind in range(4):
                    block = jnp.zeros((32, 128), F32)
                    for yb in range(4):
                        piece = turned[32 * yb : 32 * yb + 32, :]
                        shift = (32 * (yb - kind)) % 128
                        if shift:
                            piece = pltpu.roll(piece, shift, 1)
                        block = jnp.where(quarter == yb, piece, block)
                    high = block.astype(BF16)
                    rows = pl.ds((2 * s + kind % 2) * half + 32 * x, 32)
                    lanes = pl.ds(128 * group, 128)
                    a_high[kind // 2, rows, lanes] = high
                    a_low[kind // 2, rows, lanes] = (block - high.astype(F32)).astype(BF16)

    scale = 1.0 / math.sqrt(nx * ny)
    sub = lax.broadcasted_iota(jnp.int32, (8, PART), 0)
    top = sub < 4
    lane = lax.broadcasted_iota(jnp.int32, (8, 128), 1)
    first = lane < 64
    mirror = 127 - lane

    def times(a, b):
        return (a[0] * b[0] - a[1] * b[1], a[0] * b[1] + a[1] * b[0])

    @pl.loop(0, tiles)
    def _(tile):
        seed_load(tile).wait()

        @pl.when(tile == 0)
        def _():
            for load, _ in moves:
                load.start()

        @pl.when(tile == 1)
        def _():
            for load, save in moves:
                load.wait()
                save.start()

        for o in range(0, TILE, PART):
            lanes = slice(o, o + PART)
            if o == TILE // 2:
                far_save(tile, 0).start()
            for f in range(2):
                omega = 2.0 * math.pi / WAVELENGTHS[f]
                kappa = [math.cos(omega * (s + 1) * DT) * scale for s in range(2)]
                sigma = [math.sin(omega * (s + 1) * DT) * scale for s in range(2)]

                def seed(i):
                    row = 32 * f + 16 + i
                    return jnp.broadcast_to(seeds[tile, row : row + 1, lanes], (8, PART))

                v = (seeds[tile, 32 * f : 32 * f + 8, lanes], seeds[tile, 32 * f + 8 : 32 * f + 16, lanes])
                e16 = (seed(12), seed(13))
                w = times(v, (seed(10), seed(11)))
                waves = []
                for j in range(depth // 16):
                    waves += [v, w]
                    if 16 * (j + 1) < depth:
                        v, w = times(v, e16), times(w, e16)
                order = [
                    (4 * group + y) * per + yb for group in range(depth // 128) for yb in range(per) for y in range(4)
                ]
                sums = []
                for trig in range(2):
                    full = jnp.concatenate([waves[j][trig] for j in order], axis=0)
                    high = full.astype(BF16)
                    low = (full - high.astype(F32)).astype(BF16)
                    ah, al = a_high[trig], a_low[trig]
                    sums.append(jnp.dot(
                        jnp.concatenate([ah, ah, al], axis=1), jnp.concatenate([high, low, high], axis=0),
                        preferred_element_type=F32))
                w = (jnp.where(top, seed(0), seed(2)), jnp.where(top, seed(1), seed(3)))
                e2 = (seed(4), seed(5))
                acc = [[None] * 4, [None] * 4]
                for g in range(nx // 4):
                    for s in range(2):
                        for trig in range(2):
                            for odd in range(2):
                                at = (2 * s + odd) * half + 8 * g
                                term = sums[trig][at : at + 8, :] * w[odd]
                                i = 2 * trig + odd
                                acc[s][i] = term if g == 0 else acc[s][i] + term
                    if g + 1 < nx // 4:
                        w = times(w, e2)
                ck, sk, dk, rk = [acc[0][i] * kappa[0] + acc[1][i] * kappa[1] for i in range(4)]
                cg, sg, dg, rg = [acc[0][i] * sigma[0] + acc[1][i] * sigma[1] for i in range(4)]
                re_same, re_diff = ck - rk, ck + rk
                im_same, im_diff = cg - rg, cg + rg
                plus_k, minus_k = sk + dk, sk - dk
                plus_g, minus_g = sg + dg, sg - dg
                quads = (
                    (re_same + plus_g, plus_k - im_same),
                    (re_diff - minus_g, -minus_k - im_diff),
                    (re_same - plus_g, -plus_k - im_same),
                    (re_diff + minus_g, minus_k - im_diff),
                )
                same = (seed(6), jnp.where(top, -seed(7), seed(7)))
                diff = (seed(8), jnp.where(top, -seed(9), seed(9)))
                done = []
                for q, (re, im) in enumerate(quads):
                    both = jnp.where(top, re, im) + pltpu.roll(jnp.where(top, im, re), 4, 0)
                    turn = (same, diff)[q % 2]
                    swing = pltpu.roll(both, 4, 0) * turn[1]
                    done.append(both * turn[0] + (swing if q in (0, 3) else -swing))
                for pair in range(PART // 128):
                    cut = slice(128 * pair, 128 * pair + 128)
                    for h in range(2):
                        here, back = done[2 * h][:, cut], jnp.take_along_axis(done[2 * h + 1][:, cut], mirror, axis=1)
                        both = (jnp.where(first, here, back), pltpu.roll(jnp.where(first, back, here), 64, 1))
                        for t in range(2):
                            d = (2 * (o // 128 + pair) + t) * 256 + h * 128
                            far[tile, f, 0, :, d : d + 128] = both[t][0:4]
                            far[tile, f, 1, :, d : d + 128] = both[t][4:8]
        far_save(tile, 1).start()

    @pl.loop(0, tiles)
    def _(tile):
        far_save(tile, 0).wait()
        far_save(tile, 1).wait()

    for _, save in moves:
        save.wait()


def shards(
    e_field, h_field, polar, polar_prev, material,
    eps_table, delta_table, omega_table, damping_table, surface_flags,
):
    _, cx, cy, nz = e_field.shape
    ngx, ngy = lax.axis_size("gx"), lax.axis_size("gy")
    nx, ny = ngx * cx, ngy * cy
    width = 4 * nx
    hbm = pl.BlockSpec(memory_space=pl.ANY)
    field = jax.ShapeDtypeStruct(e_field.shape, F32)
    dma = pltpu.SemaphoreType.DMA
    e, h, p, g = pl.pallas_call(
        functools.partial(step_kernel, ngx, ngy, eps_table.shape[0]),
        out_shape=(field, field, field, jax.ShapeDtypeStruct((2, ngx * ngy, 8, 128), F32)),
        in_specs=[hbm] * 10,
        out_specs=(hbm,) * 4,
        scratch_shapes=[
            *[pltpu.VMEM(e_field.shape, F32)] * 4,
            pltpu.VMEM((cx, cy, nz), jnp.int32),
            pltpu.VMEM((2, 2, cy, nz), F32),
            pltpu.VMEM((2, 2, 2, cx, 1, nz), F32),
            pltpu.VMEM((2, 2, 1, nz), F32),
            pltpu.VMEM((2, 2, cy, nz), F32),
            pltpu.VMEM((2, 2, cy, nz), F32),
            pltpu.VMEM((2, 2, cx, 1, nz), F32),
            pltpu.VMEM((2, 2, cx, 1, nz), F32),
            pltpu.VMEM((2, 2, 1, nz), F32),
            pltpu.VMEM((2, 8, 128), F32),
            *[pltpu.SMEM(table.shape, F32) for table in (eps_table, delta_table, omega_table, damping_table)],
            pltpu.SMEM(surface_flags.shape, jnp.int32),
            dma((13,)), dma((5,)), *[dma((2, 2, 4))] * 2, *[dma((2, 2, 2))] * 4,
            dma((2, ngx * ngy)), dma((2, ngx * ngy)), pltpu.SemaphoreType.REGULAR,
        ],
        compiler_params=pltpu.CompilerParams(
            collective_id=0, has_side_effects=True, vmem_limit_bytes=58 * 1024 * 1024),
    )(e_field, h_field, polar, polar_prev, material,
      eps_table, delta_table, omega_table, damping_table, surface_flags)

    steps = (NDIR // 4) // TILE
    seeds = make_seeds(nx, ny)
    far, e, h, p = pl.pallas_call(
        functools.partial(far_kernel, ngx, ngy, nx, ny),
        out_shape=(jax.ShapeDtypeStruct((2, 2, 4, NDIR), F32), field, field, field),
        in_specs=[hbm] * 5,
        out_specs=(hbm,) * 4,
        scratch_shapes=[
            pltpu.VMEM(g.shape, F32),
            pltpu.VMEM(seeds.shape, F32),
            pltpu.VMEM((steps, 2, 2, 4, 4 * TILE), F32),
            pltpu.VMEM((2, 2 * width, ny // 2), BF16),
            pltpu.VMEM((2, 2 * width, ny // 2), BF16),
            *[pltpu.VMEM(e_field.shape, F32)] * 3,
            dma((2, 3)), dma((steps,)), dma((steps, 2)), dma,
        ],
        compiler_params=pltpu.CompilerParams(vmem_limit_bytes=56 * 1024 * 1024),
    )(g, jnp.asarray(seeds), e, h, p)
    return e, h, p, far


def solution(mesh):
    cells = P(None, "gx", "gy", None)
    placed = (cells, cells, cells, cells, P("gx", "gy", None), P(), P(), P(), P(), P("gx", "gy"))
    return jax.shard_map(
        shards, mesh=mesh, in_specs=placed, out_specs=(cells, cells, cells, P()), check_vma=False,
    )
```

```python
import functools
import math

import jax
import jax.numpy as jnp
import numpy as np
from jax import lax
from jax.experimental import pallas as pl
from jax.experimental.pallas import tpu as pltpu
from jax.sharding import PartitionSpec as P

NTH = 64
NPH = 256
NDIR = 16384
ZS = 384
DT = 0.55
WAVELENGTHS = (5.0, 4.0)
MESH = pl.DeviceIdType.MESH
F32 = jnp.float32
BF16 = jnp.bfloat16
BY = 8
H_PARTS = (((128, 512), (0, 128)), ((256, 512), (0, 256)))
E_PARTS = (((256, 512), (0, 256)), ((384, 512), (0, 384)))


def coefficients(nmat, nz, eps, delta, omega, damping):
    coef = []
    for m in range(nmat):
        half = jnp.full((1, nz), damping[m], F32) * (DT / 2.0)
        denom = 1.0 + half
        om = jnp.full((1, nz), omega[m], F32)
        square = om * om * (DT * DT)
        coef.append((
            (2.0 - square) / denom,
            (half - 1.0) / denom,
            jnp.full((1, nz), delta[m], F32) * square / denom,
            1.0 / jnp.full((1, nz), eps[m], F32),
        ))
    return coef


def step_kernel(
    ngx, ngy, nmat,
    e_in, h_in, p_in, q_in, m_in, eps_in, delta_in, omega_in, damping_in, flags_in,
    e_out, h_out, p_out, g_out,
    E, H, PA, PB, MAT, xstage, ystage, cstage, xe, xh, ye, yh, ce, G, eps, delta, omega, damping, flags,
    in_sem, out_sem, xs_sem, xr_sem, ys_sem, yr_sem, cs_sem, cr_sem, g1s, g1r, all_in,
):
    cx, cy, nz = MAT.shape
    gx = lax.axis_index("gx")
    gy = lax.axis_index("gy")

    inner, lower = pl.ds(1, cx - 2), pl.ds(0, cx - 1)
    pairs = [
        (e_in.at[:, 0], E.at[:, 0]), (e_in.at[:, cx - 1], E.at[:, cx - 1]), (h_in.at[:, cx - 1], H.at[:, cx - 1]),
        (e_in.at[:, inner], E.at[:, inner]), (h_in.at[:, lower], H.at[:, lower]),
        (p_in, PA), (q_in, PB), (m_in, MAT),
        (eps_in, eps), (delta_in, delta), (omega_in, omega), (damping_in, damping), (flags_in, flags),
    ]
    loads = [pltpu.make_async_copy(src, dst, in_sem.at[i]) for i, (src, dst) in enumerate(pairs)]
    for load in loads[:5] + loads[8:]:
        load.start()

    barrier = pltpu.get_barrier_semaphore()
    for k in range(1, ngx):
        pl.semaphore_signal(barrier, inc=1, device_id=(lax.rem(gx + k, ngx), gy), device_id_type=MESH)
    for k in range(1, ngy):
        pl.semaphore_signal(barrier, inc=1, device_id=(gx, lax.rem(gy + k, ngy)), device_id_type=MESH)

    for dx, dy in ((1, ngy - 1), (ngx - 1, 1)):
        pl.semaphore_signal(
            barrier, inc=1, device_id=(lax.rem(gx + dx, ngx), lax.rem(gy + dy, ngy)), device_id_type=MESH)

    not_low_x, not_high_x = gx > 0, gx < ngx - 1
    not_low_y, not_high_y = gy > 0, gy < ngy - 1
    dt_x = jnp.where(not_low_x, DT, 0.0)
    dt_y = jnp.where(not_low_y, DT, 0.0)

    def clear(ref):
        ref[...] = jnp.zeros(ref.shape, F32)

    pl.when(gx == ngx - 1)(lambda: clear(xe))
    pl.when(gx == 0)(lambda: clear(xh))
    pl.when(gy == ngy - 1)(lambda: clear(ye))
    pl.when(gy == 0)(lambda: clear(yh))
    for kind, there in ((0, not_low_x & not_high_y), (1, not_high_x & not_low_y)):

        @pl.when(jnp.logical_not(there))
        def _():
            for step in range(2):
                ce[step, kind] = jnp.zeros((1, nz), F32)

    sends_x, takes_x = (not_low_x, not_high_x), (not_high_x, not_low_x)
    sends_y, takes_y = (not_low_y, not_high_y), (not_high_y, not_low_y)

    def lanes_of(step, way, part):
        low, high = (H_PARTS, E_PARTS)[way][step][part]
        return pl.ds(low, high - low)

    def x_copies(step, way, part):
        lanes = lanes_of(step, way, part)
        src = E.at[pl.ds(1, 2), 0, :, lanes] if way == 0 else xstage.at[step, :, :, lanes]
        return [pltpu.make_async_remote_copy(
            src_ref=src, dst_ref=(xe, xh)[way].at[step, :, :, lanes],
            send_sem=xs_sem.at[step, way, part], recv_sem=xr_sem.at[step, way, part],
            device_id=(lax.rem(gx + (ngx - 1, 1)[way], ngx), gy), device_id_type=MESH)]

    def y_copy(step, way, part):
        lanes = lanes_of(step, way, part)
        return pltpu.make_async_remote_copy(
            src_ref=ystage.at[step, way, :, :, :, lanes], dst_ref=(ye, yh)[way].at[step, :, :, :, lanes],
            send_sem=ys_sem.at[step, way, part], recv_sem=yr_sem.at[step, way, part],
            device_id=(gx, lax.rem(gy + (ngy - 1, 1)[way], ngy)), device_id_type=MESH)

    sends_c = (not_high_x & not_low_y, not_low_x & not_high_y)
    takes_c = (not_low_x & not_high_y, not_high_x & not_low_y)

    def c_copy(step, kind, part):
        dx, dy = ((1, ngy - 1), (ngx - 1, 1))[kind]
        lanes = lanes_of(step, 1, part)
        return pltpu.make_async_remote_copy(
            src_ref=cstage.at[step, kind, :, lanes], dst_ref=ce.at[step, kind, :, lanes],
            send_sem=cs_sem.at[step, kind, part], recv_sem=cr_sem.at[step, kind, part],
            device_id=(lax.rem(gx + dx, ngx), lax.rem(gy + dy, ngy)), device_id_type=MESH)

    def send_x(step, way, part):
        @pl.when(sends_x[way])
        def _():
            for copy in x_copies(step, way, part):
                copy.start()

    def take_x(step, way, part):
        @pl.when(takes_x[way])
        def _():
            for copy in x_copies(step, way, part):
                copy.wait_recv()

    def sent_x(step, way, part):
        @pl.when(sends_x[way])
        def _():
            for copy in x_copies(step, way, part):
                copy.wait_send()

    def send_y(step, way, part):
        pl.when(sends_y[way])(lambda: y_copy(step, way, part).start())

    def take_y(step, way, part):
        pl.when(takes_y[way])(lambda: y_copy(step, way, part).wait_recv())

    def sent_y(step, way, part):
        pl.when(sends_y[way])(lambda: y_copy(step, way, part).wait_send())

    def send_c(step, part):
        lanes = slice(*E_PARTS[step][part])
        cstage[step, 0, :, lanes] = E[0, cx - 1, 0:1, lanes]
        cstage[step, 1, :, lanes] = E[1, 0, cy - 1 : cy, lanes]
        for kind in range(2):
            pl.when(sends_c[kind])(lambda: c_copy(step, kind, part).start())

    def take_c(step, kind, part):
        pl.when(takes_c[kind])(lambda: c_copy(step, kind, part).wait_recv())

    def sent_c(step, kind, part):
        pl.when(sends_c[kind])(lambda: c_copy(step, kind, part).wait_send())

    blocks = range(cy // BY)
    last = cy // BY - 1

    def ids(span, dim):
        return lax.broadcasted_iota(jnp.int32, (BY, span[1] - span[0]), dim)

    def up_y(v, row, span):
        return jnp.where(ids(span, 0) == BY - 1, row, pltpu.roll(v, BY - 1, 0))

    def down_y(v, row, span):
        return jnp.where(ids(span, 0) == 0, row, pltpu.roll(v, 1, 0))

    def up_z(ref, c, x, here, span):
        low, high = span
        n = high - low
        if high == nz:
            return jnp.where(ids(span, 1) == n - 1, 0.0, pltpu.roll(ref[c, x, here, low:high], n - 1, 1))
        return pltpu.roll(ref[c, x, here, low : high + 128], n + 127, 1)[:, :n]

    def down_z(ref, c, x, here, span):
        low, high = span
        if low == 0:
            return jnp.where(ids(span, 1) == 0, 0.0, pltpu.roll(ref[c, x, here, low:high], 1, 1))
        return pltpu.roll(ref[c, x, here, low - 128 : high], 1, 1)[:, 128:]

    def part_x(step, part):
        span = E_PARTS[step][part]
        lanes, x = slice(*span), cx - 1
        for block in blocks:
            here, y = pl.ds(block * BY, BY), block * BY
            ex, ey, ez = E[0, x, here, lanes], E[1, x, here, lanes], E[2, x, here, lanes]
            rx = E[0, x, y + BY : y + BY + 1, lanes] if block < last else jnp.zeros((1, span[1] - span[0]), F32)
            xstage[step, 0, here, lanes] = H[1, x, here, lanes] - DT * ((up_z(E, 0, x, here, span) - ex) + ez)
            xstage[step, 1, here, lanes] = H[2, x, here, lanes] + DT * (ey + (up_y(ex, rx, span) - ex))
        send_x(step, 1, part)

    def part_y(step, part):
        span = E_PARTS[step][part]
        here, lanes = pl.ds(cy - BY, BY), slice(*span)
        for x in range(cx):
            ex, ey, ez = E[0, x, here, lanes], E[1, x, here, lanes], E[2, x, here, lanes]
            slope = E[1, x + 1, here, lanes] - ey if x < cx - 1 else -ey
            part_hx = H[0, x, here, lanes] + DT * (ez + (up_z(E, 1, x, here, span) - ey))
            part_hz = H[2, x, here, lanes] - DT * (slope + ex)
            ystage[step, 1, 0, x, :, lanes] = part_hx[BY - 1 : BY, :]
            ystage[step, 1, 1, x, :, lanes] = part_hz[BY - 1 : BY, :]
        send_y(step, 1, part)

    def rows_y(step, part):
        lanes = slice(*H_PARTS[step][part])
        for i, c in enumerate((0, 2)):
            for x in range(cx):
                ystage[step, 0, i, x, :, lanes] = E[c, x, 0:1, lanes]
        send_y(step, 0, part)

    def h_plane(step, x, blocks, span):
        lanes = slice(*span)
        for y in [BY * block for block in blocks]:
            here = pl.ds(y, BY)
            ex, ey, ez = E[0, x, here, lanes], E[1, x, here, lanes], E[2, x, here, lanes]
            if y + BY < cy:
                rx, rz = E[0, x, y + BY : y + BY + 1, lanes], E[2, x, y + BY : y + BY + 1, lanes]
            else:
                rx, rz = ye[step, 0, x, :, lanes], ye[step, 1, x, :, lanes]
            if isinstance(x, int) and x == cx - 1:
                eyx, ezx = xe[step, 0, here, lanes], xe[step, 1, here, lanes]
            else:
                eyx, ezx = E[1, x + 1, here, lanes], E[2, x + 1, here, lanes]
            curl_x = (up_y(ez, rz, span) - ez) - (up_z(E, 1, x, here, span) - ey)
            curl_y = (up_z(E, 0, x, here, span) - ex) - (ezx - ez)
            curl_z = (eyx - ey) - (up_y(ex, rx, span) - ex)
            H[0, x, here, lanes] = H[0, x, here, lanes] - DT * curl_x
            H[1, x, here, lanes] = H[1, x, here, lanes] - DT * curl_y
            H[2, x, here, lanes] = H[2, x, here, lanes] - DT * curl_z

    def e_plane(step, x, coef, blocks, span):
        now, old = (PA, PB) if step == 0 else (PB, PA)
        fixed = isinstance(x, int)
        lanes, n = slice(*span), span[1] - span[0]
        for y in [BY * block for block in blocks]:
            here = pl.ds(y, BY)
            mat = MAT[x, here, lanes]
            vox = [jnp.broadcast_to(coef[nmat - 1][i][:, :n], (BY, n)) for i in range(4)]
            for m in range(nmat - 1):
                hit = mat == m
                vox = [jnp.where(hit, coef[m][i][:, :n], vox[i]) for i in range(4)]
            a, b, c, inv = vox
            hx, hy, hz = H[0, x, here, lanes], H[1, x, here, lanes], H[2, x, here, lanes]
            if y > 0:
                rx, rz = H[0, x, y - 1 : y, lanes], H[2, x, y - 1 : y, lanes]
            else:
                rx = yh[step, 0, x, :, lanes] - dt_y * E[2, x, 0:1, lanes]
                edge = E[0, x, 0:1, lanes]
                if fixed and x == cx - 1:
                    edge = edge - ce[step, 1, :, lanes]
                rz = yh[step, 1, x, :, lanes] + dt_y * edge
            if fixed and x == 0:
                hyx = xh[step, 0, here, lanes] + dt_x * E[2, 0, here, lanes]
                edge = E[1, 0, here, lanes]
                if y + BY == cy:
                    edge = jnp.where(ids(span, 0) == BY - 1, edge - ce[step, 0, :, lanes], edge)
                hzx = xh[step, 1, here, lanes] - dt_x * edge
            else:
                hyx, hzx = H[1, x - 1, here, lanes], H[2, x - 1, here, lanes]
            curls = (
                (hz - down_y(hz, rz, span)) - (hy - down_z(H, 1, x, here, span)),
                (hx - down_z(H, 0, x, here, span)) - (hz - hzx),
                (hy - hyx) - (hx - down_y(hx, rx, span)),
            )
            for i in range(3):
                e, p = E[i, x, here, lanes], now[i, x, here, lanes]
                new = a * p + b * old[i, x, here, lanes] + c * e
                E[i, x, here, lanes] = e + (DT * curls[i] - (new - p)) * inv
                old[i, x, here, lanes] = new

    me = gx * ngy + gy
    count = ngx * ngy
    turn_x, turn_y = 2 * gx >= ngx, 2 * gy >= ngy
    tile_lane = lax.broadcasted_iota(jnp.int32, (8, 128), 1)
    tile_row = lax.broadcasted_iota(jnp.int32, (8, 128), 0)

    def surface(step, flag):
        def body(x, acc):
            at = jnp.where(turn_x, cx - 1 - x, x) * 4
            for yb in range(cy // 8):
                base = jnp.where(turn_y, cy // 8 - 1 - yb, yb) * (4 * cx) + at
                rows = slice(8 * yb, 8 * yb + 8)
                cols = (
                    -H[1, x, rows, ZS : ZS + 1], H[0, x, rows, ZS : ZS + 1],
                    E[1, x, rows, ZS : ZS + 1], -E[0, x, rows, ZS : ZS + 1],
                )
                for j in range(4):
                    acc = jnp.where(tile_lane == base + j, cols[j], acc)
            return acc

        tile = lax.fori_loop(0, cx, body, jnp.zeros((8, 128), F32)) * flag
        back = tile
        for bit in (1, 2, 4):
            back = jnp.where((tile_row & bit) != 0, pltpu.roll(back, bit, 0), pltpu.roll(back, 8 - bit, 0))
        G[step] = jnp.where(turn_y, back, tile)

    def peer(step, k):
        to = lax.rem(me + k, count)
        return pltpu.make_async_remote_copy(
            src_ref=G.at[step], dst_ref=g_out.at[step, me], send_sem=g1s.at[step, k], recv_sem=g1r.at[step, k],
            device_id=(to // ngy, lax.rem(to, ngy)), device_id_type=MESH)

    def own(step):
        return pltpu.make_async_copy(G.at[step], g_out.at[step, me], out_sem.at[3 + step])

    def gather_start(step):
        own(step).start()

        for k in range(1, count):
            peer(step, k).start()

    def gather_end(step):
        own(step).wait()

        @pl.loop(1, count)
        def _(k):
            peer(step, k).wait()

    every = (0, nz)
    loads[0].wait()
    pl.semaphore_wait(barrier, ngx + ngy)
    send_x(0, 0, 0)
    loads[1].wait()
    send_c(0, 0)
    loads[2].wait()
    part_x(0, 0)
    send_x(0, 0, 1)
    loads[3].wait()
    rows_y(0, 0)
    loads[4].wait()
    for load in loads[5:8]:
        load.start()
    part_y(0, 0)
    send_c(0, 1)
    part_x(0, 1)
    rows_y(0, 1)
    part_y(0, 1)
    for k in range(1, ngy):
        pl.semaphore_signal(all_in, inc=1, device_id=(gx, lax.rem(gy + k, ngy)), device_id_type=MESH)
    for load in loads[8:]:
        load.wait()

    coef = coefficients(nmat, nz, eps, delta, omega, damping)
    flag = flags[0, 0].astype(F32)

    for step in range(2):

        @pl.loop(0, cx - 1)
        def _(x):
            h_plane(step, x, range(last), every)

        if step == 0:
            for load in loads[5:8]:
                load.wait()
        else:
            gather_start(0)

        @pl.loop(1, cx - 1)
        def _(x):
            e_plane(step, x, coef, range(1, last), every)

        for part in range(2):
            h_span, e_span = H_PARTS[step][part], E_PARTS[step][part]
            take_y(step, 0, part)

            @pl.loop(0, cx - 1)
            def _(x):
                h_plane(step, x, [last], h_span)

            take_x(step, 0, part)
            h_plane(step, cx - 1, blocks, h_span)
            if step == 1 and part == 1:
                pltpu.make_async_copy(H, h_out, out_sem.at[0]).start()
            sent_x(step, 0, part)
            take_y(step, 1, part)
            take_c(step, 1, part)
            e_plane(step, cx - 1, coef, blocks, e_span)
            if step == 0:
                part_x(1, part)
            take_x(step, 1, part)
            take_c(step, 0, part)
            e_plane(step, 0, coef, blocks, e_span)
            if step == 0:
                send_x(1, 0, part)
                send_c(1, part)

            @pl.loop(1, cx - 1)
            def _(x):
                e_plane(step, x, coef, [0, last], e_span)

            if step == 0:
                rows_y(1, part)
                part_y(1, part)
            elif part == 0:
                surface(1, flag)
                gather_start(1)
        if step == 0:
            surface(0, flag)
            pl.semaphore_wait(all_in, ngy - 1)

    saves = [
        pltpu.make_async_copy(H, h_out, out_sem.at[0]),
        pltpu.make_async_copy(E, e_out, out_sem.at[1]),
        pltpu.make_async_copy(PA, p_out, out_sem.at[2]),
    ]
    saves[1].start()
    saves[2].start()
    for step in range(2):
        for part in range(2):
            sent_x(step, 1, part)
            for i in range(2):
                sent_y(step, i, part)
                sent_c(step, i, part)
    gather_end(0)
    gather_end(1)
    for save in saves:
        save.wait()


TILE = 2048
PART = 256


def angles():
    theta = (np.arange(NTH, dtype=np.float64)[:, None] + 0.5) * (math.pi / 2.0 / NTH)
    phi = (np.arange(NPH // 4, dtype=np.float64)[None, :] + 0.5) * (2.0 * math.pi / NPH)
    ux = (np.sin(theta) * np.cos(phi)).reshape(-1)
    uy = (np.sin(theta) * np.sin(phi)).reshape(-1)
    return ux, uy


def tiled(rows):
    return np.ascontiguousarray(rows.reshape(rows.shape[0], -1, TILE).swapaxes(0, 1))


def make_seeds(nx, ny):
    ux, uy = angles()
    x0, y0 = (nx - 1) / 2.0, (ny - 1) / 2.0
    rows = []
    for length in WAVELENGTHS:
        wave = 2.0 * math.pi / length
        turns = [(y0 - y) * uy for y in range(8)]
        rows += [np.cos(wave * angle) for angle in turns] + [np.sin(wave * angle) for angle in turns]
        for angle in (x0 * ux, (x0 - 1.0) * ux, -2.0 * ux, x0 * ux + y0 * uy, x0 * ux - y0 * uy, -8.0 * uy, -16.0 * uy):
            rows += [np.cos(wave * angle), np.sin(wave * angle)]
        rows += [np.zeros_like(ux)] * 2
    return tiled(np.stack(rows).astype(np.float32))


def far_kernel(
    ngx, ngy, nx, ny, g_in, seeds_in, e_in, h_in, p_in, far_out, e_out, h_out, p_out,
    g_ref, seeds, far, a_high, a_low, e_pass, h_pass, p_pass, sem, seed_sem, far_sem, g_sem,
):
    half = 2 * nx
    depth = ny // 2
    per = ny // ngy // 8
    tiles = seeds.shape[0]
    g_load = pltpu.make_async_copy(g_in, g_ref, g_sem)
    g_load.start()

    def seed_load(tile):
        return pltpu.make_async_copy(seeds_in.at[tile], seeds.at[tile], seed_sem.at[tile])

    def far_save(tile, i):
        lanes = pl.ds(pl.multiple_of(tile * 4 * TILE + i * 2 * TILE, 2 * TILE), 2 * TILE)
        src = far.at[tile, :, :, :, pl.ds(i * 2 * TILE, 2 * TILE)]
        return pltpu.make_async_copy(src, far_out.at[:, :, :, lanes], far_sem.at[tile, i])

    for tile in range(tiles):
        seed_load(tile).start()
    fields = enumerate(zip((e_in, h_in, p_in), (e_pass, h_pass, p_pass), (e_out, h_out, p_out)))
    moves = [
        (pltpu.make_async_copy(src, mid, sem.at[0, i]), pltpu.make_async_copy(mid, dst, sem.at[1, i]))
        for i, (src, mid, dst) in fields
    ]
    g_load.wait()
    quarter = lax.broadcasted_iota(jnp.int32, (32, 128), 1) // 32
    for s in range(2):
        for x in range(ngx // 2):
            for group in range(ngy // 8):
                kinds = [[], [], [], []]
                for y in range(4 * group, 4 * group + 4):
                    low_x, high_x = x * ngy, (ngx - 1 - x) * ngy
                    t00, t10 = g_ref[s, low_x + y], g_ref[s, high_x + y]
                    t01, t11 = g_ref[s, low_x + ngy - 1 - y], g_ref[s, high_x + ngy - 1 - y]
                    even0, even1, odd0, odd1 = t10 + t00, t11 + t01, t10 - t00, t11 - t01
                    for kind, tile in zip(kinds, (even0 + even1, odd0 + odd1, even1 - even0, odd1 - odd0)):
                        kind.append(tile)
                turned = jnp.concatenate(kinds[0] + kinds[1] + kinds[2] + kinds[3], axis=0).T
                for kind in range(4):
                    block = jnp.zeros((32, 128), F32)
                    for yb in range(4):
                        piece = turned[32 * yb : 32 * yb + 32, :]
                        shift = (32 * (yb - kind)) % 128
                        if shift:
                            piece = pltpu.roll(piece, shift, 1)
                        block = jnp.where(quarter == yb, piece, block)
                    high = block.astype(BF16)
                    rows = pl.ds((2 * s + kind % 2) * half + 32 * x, 32)
                    lanes = pl.ds(128 * group, 128)
                    a_high[kind // 2, rows, lanes] = high
                    a_low[kind // 2, rows, lanes] = (block - high.astype(F32)).astype(BF16)

    scale = 1.0 / math.sqrt(nx * ny)
    sub = lax.broadcasted_iota(jnp.int32, (8, PART), 0)
    top = sub < 4
    lane = lax.broadcasted_iota(jnp.int32, (8, 128), 1)
    first = lane < 64
    mirror = 127 - lane

    def times(a, b):
        return (a[0] * b[0] - a[1] * b[1], a[0] * b[1] + a[1] * b[0])

    @pl.loop(0, tiles)
    def _(tile):
        seed_load(tile).wait()

        @pl.when(tile == 0)
        def _():
            for load, _ in moves:
                load.start()

        @pl.when(tile == 1)
        def _():
            for load, save in moves:
                load.wait()
                save.start()

        for o in range(0, TILE, PART):
            lanes = slice(o, o + PART)
            if o == TILE // 2:
                far_save(tile, 0).start()
            for f in range(2):
                omega = 2.0 * math.pi / WAVELENGTHS[f]
                kappa = [math.cos(omega * (s + 1) * DT) * scale for s in range(2)]
                sigma = [math.sin(omega * (s + 1) * DT) * scale for s in range(2)]

                def seed(i):
                    row = 32 * f + 16 + i
                    return jnp.broadcast_to(seeds[tile, row : row + 1, lanes], (8, PART))

                v = (seeds[tile, 32 * f : 32 * f + 8, lanes], seeds[tile, 32 * f + 8 : 32 * f + 16, lanes])
                e16 = (seed(12), seed(13))
                w = times(v, (seed(10), seed(11)))
                waves = []
                for j in range(depth // 16):
                    waves += [v, w]
                    if 16 * (j + 1) < depth:
                        v, w = times(v, e16), times(w, e16)
                order = [
                    (4 * group + y) * per + yb for group in range(depth // 128) for yb in range(per) for y in range(4)
                ]
                sums = []
                for trig in range(2):
                    full = jnp.concatenate([waves[j][trig] for j in order], axis=0)
                    high = full.astype(BF16)
                    low = (full - high.astype(F32)).astype(BF16)
                    ah, al = a_high[trig], a_low[trig]
                    sums.append(jnp.dot(
                        jnp.concatenate([ah, ah, al], axis=1), jnp.concatenate([high, low, high], axis=0),
                        preferred_element_type=F32))
                w = (jnp.where(top, seed(0), seed(2)), jnp.where(top, seed(1), seed(3)))
                e2 = (seed(4), seed(5))
                acc = [[None] * 4, [None] * 4]
                for g in range(nx // 4):
                    for s in range(2):
                        for trig in range(2):
                            for odd in range(2):
                                at = (2 * s + odd) * half + 8 * g
                                term = sums[trig][at : at + 8, :] * w[odd]
                                i = 2 * trig + odd
                                acc[s][i] = term if g == 0 else acc[s][i] + term
                    if g + 1 < nx // 4:
                        w = times(w, e2)
                ck, sk, dk, rk = [acc[0][i] * kappa[0] + acc[1][i] * kappa[1] for i in range(4)]
                cg, sg, dg, rg = [acc[0][i] * sigma[0] + acc[1][i] * sigma[1] for i in range(4)]
                re_same, re_diff = ck - rk, ck + rk
                im_same, im_diff = cg - rg, cg + rg
                plus_k, minus_k = sk + dk, sk - dk
                plus_g, minus_g = sg + dg, sg - dg
                quads = (
                    (re_same + plus_g, plus_k - im_same),
                    (re_diff - minus_g, -minus_k - im_diff),
                    (re_same - plus_g, -plus_k - im_same),
                    (re_diff + minus_g, minus_k - im_diff),
                )
                same = (seed(6), jnp.where(top, -seed(7), seed(7)))
                diff = (seed(8), jnp.where(top, -seed(9), seed(9)))
                done = []
                for q, (re, im) in enumerate(quads):
                    both = jnp.where(top, re, im) + pltpu.roll(jnp.where(top, im, re), 4, 0)
                    turn = (same, diff)[q % 2]
                    swing = pltpu.roll(both, 4, 0) * turn[1]
                    done.append(both * turn[0] + (swing if q in (0, 3) else -swing))
                for pair in range(PART // 128):
                    cut = slice(128 * pair, 128 * pair + 128)
                    for h in range(2):
                        here, back = done[2 * h][:, cut], jnp.take_along_axis(done[2 * h + 1][:, cut], mirror, axis=1)
                        both = (jnp.where(first, here, back), pltpu.roll(jnp.where(first, back, here), 64, 1))
                        for t in range(2):
                            d = (2 * (o // 128 + pair) + t) * 256 + h * 128
                            far[tile, f, 0, :, d : d + 128] = both[t][0:4]
                            far[tile, f, 1, :, d : d + 128] = both[t][4:8]
        far_save(tile, 1).start()

    @pl.loop(0, tiles)
    def _(tile):
        far_save(tile, 0).wait()
        far_save(tile, 1).wait()

    for _, save in moves:
        save.wait()


def shards(
    e_field, h_field, polar, polar_prev, material,
    eps_table, delta_table, omega_table, damping_table, surface_flags,
):
    _, cx, cy, nz = e_field.shape
    ngx, ngy = lax.axis_size("gx"), lax.axis_size("gy")
    nx, ny = ngx * cx, ngy * cy
    width = 4 * nx
    hbm = pl.BlockSpec(memory_space=pl.ANY)
    field = jax.ShapeDtypeStruct(e_field.shape, F32)
    dma = pltpu.SemaphoreType.DMA
    e, h, p, g = pl.pallas_call(
        functools.partial(step_kernel, ngx, ngy, eps_table.shape[0]),
        out_shape=(field, field, field, jax.ShapeDtypeStruct((2, ngx * ngy, 8, 128), F32)),
        in_specs=[hbm] * 10,
        out_specs=(hbm,) * 4,
        scratch_shapes=[
            *[pltpu.VMEM(e_field.shape, F32)] * 4,
            pltpu.VMEM((cx, cy, nz), jnp.int32),
            pltpu.VMEM((2, 2, cy, nz), F32),
            pltpu.VMEM((2, 2, 2, cx, 1, nz), F32),
            pltpu.VMEM((2, 2, 1, nz), F32),
            pltpu.VMEM((2, 2, cy, nz), F32),
            pltpu.VMEM((2, 2, cy, nz), F32),
            pltpu.VMEM((2, 2, cx, 1, nz), F32),
            pltpu.VMEM((2, 2, cx, 1, nz), F32),
            pltpu.VMEM((2, 2, 1, nz), F32),
            pltpu.VMEM((2, 8, 128), F32),
            *[pltpu.SMEM(table.shape, F32) for table in (eps_table, delta_table, omega_table, damping_table)],
            pltpu.SMEM(surface_flags.shape, jnp.int32),
            dma((13,)), dma((5,)), *[dma((2, 2, 4))] * 2, *[dma((2, 2, 2))] * 4,
            dma((2, ngx * ngy)), dma((2, ngx * ngy)), pltpu.SemaphoreType.REGULAR,
        ],
        compiler_params=pltpu.CompilerParams(
            collective_id=0, has_side_effects=True, vmem_limit_bytes=58 * 1024 * 1024),
    )(e_field, h_field, polar, polar_prev, material,
      eps_table, delta_table, omega_table, damping_table, surface_flags)

    steps = (NDIR // 4) // TILE
    seeds = make_seeds(nx, ny)
    far, e, h, p = pl.pallas_call(
        functools.partial(far_kernel, ngx, ngy, nx, ny),
        out_shape=(jax.ShapeDtypeStruct((2, 2, 4, NDIR), F32), field, field, field),
        in_specs=[hbm] * 5,
        out_specs=(hbm,) * 4,
        scratch_shapes=[
            pltpu.VMEM(g.shape, F32),
            pltpu.VMEM(seeds.shape, F32),
            pltpu.VMEM((steps, 2, 2, 4, 4 * TILE), F32),
            pltpu.VMEM((2, 2 * width, ny // 2), BF16),
            pltpu.VMEM((2, 2 * width, ny // 2), BF16),
            *[pltpu.VMEM(e_field.shape, F32)] * 3,
            dma((2, 3)), dma((steps,)), dma((steps, 2)), dma,
        ],
        compiler_params=pltpu.CompilerParams(vmem_limit_bytes=56 * 1024 * 1024),
    )(g, jnp.asarray(seeds), e, h, p)
    return e, h, p, far


def solution(mesh):
    cells = P(None, "gx", "gy", None)
    placed = (cells, cells, cells, cells, P("gx", "gy", None), P(), P(), P(), P(), P("gx", "gy"))
    return jax.shard_map(
        shards, mesh=mesh, in_specs=placed, out_specs=(cells, cells, cells, P()), check_vma=False,
    )
```
